32 devices in a mesh: groups: 2 (over x), fsdp: 16 (over z, y, core).
Axes of the slice: x: 2, y: 2, z: 4, core: 2. Of those that a mesh axis runs over, the one named last changes fastest.
Arguments:
- activations: bfloat16 [8192, 8192], P(('groups', 'fsdp')), parts along dimension 0, may hold values from -6 to 6
- quant_codes: bfloat16 [8192, 512], P('fsdp'), may hold values from -120 to 120, as said below
- block_scales: float32 [64, 4], P('fsdp'), may hold values from 0.00012 to 0.0012
- lowrank_down_factor: bfloat16 [16384, 64], P('groups'), parts along dimension 0, may hold values from -0.0625 to 0.0625
- lowrank_up_factor: bfloat16 [128, 512], P('groups'), parts along dimension 0, may hold values from -0.75 to 0.75
- cotangent: bfloat16 [8192, 512], P(('groups', 'fsdp')), parts along dimension 0, may hold values from -6 to 6
Outputs:
- projected: bfloat16 [8192, 512], P(('groups', 'fsdp')), parts along dimension 0
- input_gradient: bfloat16 [8192, 8192], P(('groups', 'fsdp')), parts along dimension 0
- grad_down: float32 [16384, 64], P(('groups', 'fsdp')), parts along dimension 0
- grad_up: float32 [128, 512], P('groups'), parts along dimension 0
The draws below stay inside these ranges and needn't reach their ends.
There are 2 independent parts, one for each index of `groups`. The reference program is written for one: setup_inputs(seed, part) draws one part's arguments, and reference() takes and returns one part's arrays. A program takes and returns all parts, laid end to end along the dimension named above; an argument that names none is the same for every part. Nothing has to cross between parts.
Inputs may be any that keep to these rules, and one draw needn't show every extreme that they name: `quant_codes`: every entry is a value of the FP8 E4M3 grid.
All inputs are finite; a program needn't handle non-finite values.
Results may differ from the reference program's by a relative error of at most 0.0051.
Values may be sent and summed in bfloat16 or wider, within the bound.
No kernel may reach another device: no remote copies, remote signals or barrier semaphores. Data moves between devices by JAX's collectives and lax.ppermute only.
A program may use at most 64 MiB of HBM per device.

```python
import math
import jax
import jax.numpy as jnp
from jax import lax

D = 8192
NV = 512
RANK = 64
BLOCK = 128
REPLICA_TOKENS = 4096


def draw_quant_codes(key, part):
    key = jax.random.fold_in(key, 7)
    key_mantissa, key_first, key_second, key_polarity = jax.random.split(key, 4)
    extent = (D, NV)
    mantissa = jax.random.randint(key_mantissa, extent, 8, 16)
    exponent = jax.random.randint(key_first, extent, 0, 4) + jax.random.randint(key_second, extent, 0, 4)
    polarity = 2 * jax.random.randint(key_polarity, extent, 0, 2) - 1
    powered = jnp.left_shift(jnp.ones_like(exponent), exponent)
    drawn = (polarity * mantissa * powered).astype(jnp.float32) / 8.0
    return drawn.astype(jnp.bfloat16)


def with_spikes(array, own_key, source, target, blocks, factor):
    def block_of(position):
        return (jnp.arange(array.shape[position]) // (array.shape[position] // blocks)).reshape((-1,) + (1,) * (array.ndim - 1 - position))

    first = jax.random.permutation(own_key, blocks)[block_of(target)]
    second = (block_of(target) + blocks // 2) % blocks
    return jnp.where((block_of(source) == first) | (block_of(source) == second), factor * array, array)


def block_scale(own_key, shape, shards, low, high):
    def one(dim, shards_of):
        heights = jax.random.uniform(jax.random.fold_in(jax.random.fold_in(own_key, 6), dim), (shards_of,), jnp.float32, low / len(shards), high / len(shards))
        return jnp.repeat(jnp.exp(heights), shape[dim] // shards_of).reshape((-1,) + (1,) * (len(shape) - dim - 1))

    factor_of = one(*shards[0])
    for cut in shards[1:]:
        factor_of = factor_of * one(*cut)
    return factor_of


def centred(stream_key, shape, scale, most, pieces=(), held_as=jnp.bfloat16):
    entries = jax.random.normal(stream_key, shape, jnp.float32) * scale
    if len(pieces) > 0:
        entries = block_scale(stream_key, shape, pieces, -0.22, 0.18) * entries
    return jnp.clip(entries, min=-most, max=most).astype(held_as)


def noise_with(stream_key, dims, deviation, reach, cuts, heavy, kind=jnp.bfloat16):
    values = deviation * jax.random.normal(stream_key, dims, jnp.float32)
    if cuts:
        values = values * block_scale(stream_key, dims, cuts, -0.22, 0.18)
    return jnp.clip(with_spikes(values, jax.random.fold_in(stream_key, 3), *heavy), -reach, reach).astype(kind)


def setup_inputs(seed: int = 0, part: int = 0) -> dict:
    arg_keys = jax.random.split(jax.random.key(seed), 7)
    own_keys = jax.random.split(jax.random.fold_in(arg_keys[6], part), 7)
    return {
        "activations": noise_with(own_keys[0], (REPLICA_TOKENS, D), 1.0, 6.0, ((0, 16),), (0, 1, 16, 2.0)),
        "quant_codes": draw_quant_codes(jax.random.fold_in(arg_keys[6], 71), part),
        "block_scales": jnp.clip(jnp.exp(math.log(0.0012) - 2.3025852 * jax.random.uniform(arg_keys[2], (D // BLOCK, NV // BLOCK), jnp.float32) ** block_scale(arg_keys[2], (D // BLOCK, NV // BLOCK), ((0, 16),), -0.2, 0.2)), 0.00012, 0.0012),
        "lowrank_down_factor": centred(own_keys[3], (D, RANK), D ** -0.5, 0.0625),
        "lowrank_up_factor": centred(own_keys[4], (RANK, NV), RANK ** -0.5, 0.75),
        "cotangent": centred(own_keys[5], (REPLICA_TOKENS, NV), 1.0, 6.0, ((0, 16),)),
    }


lowrank_scale = 0.5

def weight_transpose(left, right):
    return lax.dot_general(left, right, (((1,), (1,)), ((), ())), preferred_element_type=jnp.float32)

def leading(left, right):
    return lax.dot_general(left, right, (((0,), (0,)), ((), ())), preferred_element_type=jnp.float32)

def reference(activations, quant_codes, block_scales, lowrank_down_factor, lowrank_up_factor, cotangent):
    spread_scales = jnp.repeat(jnp.repeat(block_scales, BLOCK, axis=0), BLOCK, axis=1)
    value_weight = (quant_codes.astype(jnp.float32) * spread_scales).astype(jnp.bfloat16)
    lowrank_hidden = jnp.dot(activations, lowrank_down_factor, preferred_element_type=jnp.float32).astype(jnp.bfloat16)
    projected = (jnp.dot(activations, value_weight, preferred_element_type=jnp.float32) + lowrank_scale * jnp.dot(lowrank_hidden, lowrank_up_factor, preferred_element_type=jnp.float32)).astype(jnp.bfloat16)
    hidden_gradient = weight_transpose(cotangent, lowrank_up_factor).astype(jnp.bfloat16)
    input_gradient = (weight_transpose(cotangent, value_weight) + lowrank_scale * weight_transpose(hidden_gradient, lowrank_down_factor)).astype(jnp.bfloat16)
    scaling_factor = lowrank_scale / math.sqrt(REPLICA_TOKENS)
    grad_down = scaling_factor * leading(activations, hidden_gradient)
    grad_up = scaling_factor * leading(lowrank_hidden, cotangent)
    return (projected, input_gradient, grad_down, grad_up)
```

```python
import math

import jax
import jax.numpy as jnp
from jax import lax
from jax.experimental import pallas as pl
from jax.experimental.pallas import tpu as pltpu
from jax.sharding import PartitionSpec as P

BLOCK = 128
AXES = ("groups", "fsdp")

lowrank_scale = 0.5


def weight_transpose(left, right):
    return lax.dot_general(
        left, right, (((1,), (1,)), ((), ())), preferred_element_type=jnp.float32
    )


def leading(left, right):
    return lax.dot_general(
        left, right, (((0,), (0,)), ((), ())), preferred_element_type=jnp.float32
    )


def dequantize(quant_codes, block_scales):
    spread_scales = jnp.repeat(jnp.repeat(block_scales, BLOCK, axis=0), BLOCK, axis=1)
    return (quant_codes.astype(jnp.float32) * spread_scales).astype(jnp.bfloat16)


def per_device_general(
    activations, quant_codes, block_scales, lowrank_down_factor, lowrank_up_factor, cotangent
):
    value_weight = dequantize(quant_codes, block_scales)
    lowrank_hidden = jnp.dot(
        activations, lowrank_down_factor, preferred_element_type=jnp.float32
    ).astype(jnp.bfloat16)
    lowrank_update = lowrank_scale * jnp.dot(
        lowrank_hidden, lowrank_up_factor, preferred_element_type=jnp.float32
    )
    hidden_gradient = weight_transpose(cotangent, lowrank_up_factor).astype(jnp.bfloat16)
    gathered = lax.all_gather(value_weight, "fsdp", axis=0, tiled=True)
    projected = (
        lowrank_update + jnp.dot(activations, gathered, preferred_element_type=jnp.float32)
    ).astype(jnp.bfloat16)
    input_gradient = (
        weight_transpose(cotangent, gathered)
        + lowrank_scale * weight_transpose(hidden_gradient, lowrank_down_factor)
    ).astype(jnp.bfloat16)
    scaling_factor = lowrank_scale / math.sqrt(activations.shape[0] * lax.axis_size("fsdp"))
    grad_down = lax.psum_scatter(
        scaling_factor * leading(activations, hidden_gradient),
        "fsdp",
        scatter_dimension=0,
        tiled=True,
    )
    grad_up = lax.psum(scaling_factor * leading(lowrank_hidden, cotangent), "fsdp")
    return (projected, input_gradient, grad_down, grad_up)


NZ = 4
VMEM_LIMIT = 40 * 1024 * 1024


def pairs_of(move):
    found = []
    for g in range(2):
        for z in range(NZ):
            for y in range(2):
                for c in range(2):
                    to = move(g, z, y, c)
                    found.append((index_of(g, z, y, c), index_of(*to)))
    return found


def index_of(g, z, y, c):
    return ((g * NZ + z) * 2 + y) * 2 + c


OVER_CORE = pairs_of(lambda g, z, y, c: (g, z, y, 1 - c))
OVER_Y = pairs_of(lambda g, z, y, c: (g, z, 1 - y, c))
OVER_X = pairs_of(lambda g, z, y, c: (1 - g, z, y, c))
Z_UP = pairs_of(lambda g, z, y, c: (g, (z + 1) % NZ, y, c))
Z_DOWN = pairs_of(lambda g, z, y, c: (g, (z - 1) % NZ, y, c))
Z_FAR = pairs_of(lambda g, z, y, c: (g, (z + 2) % NZ, y, c))


def send(array, pairs):
    return lax.ppermute(array, AXES, pairs)


def whole():
    return pl.BlockSpec(memory_space=pltpu.VMEM)


def scalars():
    return pl.BlockSpec(memory_space=pltpu.SMEM)


def anywhere():
    return pl.BlockSpec(memory_space=pl.ANY)


def params():
    return pltpu.CompilerParams(vmem_limit_bytes=VMEM_LIMIT)


LITTLE = pl.CostEstimate(flops=1, bytes_accessed=1, transcendentals=0)


def dequantize_halves(place, quant_codes, block_scales):
    rows, columns = quant_codes.shape
    half = rows // 2

    def kernel(place_ref, codes_ref, scales_ref, first_ref, other_ref):
        g = place_ref[0]
        for which, out_ref in ((g, first_ref), (1 - g, other_ref)):
            for i in range(half // BLOCK):
                start = pl.multiple_of(which * half + i * BLOCK, BLOCK)
                for j in range(columns // BLOCK):
                    block = codes_ref[pl.ds(start, BLOCK), j * BLOCK : (j + 1) * BLOCK]
                    scale = scales_ref[which * (half // BLOCK) + i, j]
                    out_ref[i * BLOCK : (i + 1) * BLOCK, j * BLOCK : (j + 1) * BLOCK] = (
                        block.astype(jnp.float32) * scale
                    ).astype(jnp.bfloat16)

    return pl.pallas_call(
        kernel,
        out_shape=[jax.ShapeDtypeStruct((half, columns), jnp.bfloat16)] * 2,
        in_specs=[scalars(), whole(), scalars()],
        out_specs=[whole()] * 2,
        compiler_params=params(),
        cost_estimate=LITTLE,
        name="dequantize",
    )(place, quant_codes, block_scales)


def local_gradients(place, activations, down_t, up, cotangent):
    tokens, width = activations.shape
    rank, features = up.shape
    chips = NZ * 2
    chunk = width // chips
    part = chunk // 2
    up_part = features // 2
    packed = chips * part + up_part

    def kernel(
        place_ref, act_ref, down_ref, up_ref, cot_ref, latent_ref, lgrad_ref, own_ref, away_ref,
        total, lgrad_t,
    ):
        step = pl.program_id(0)
        y, c = place_ref[2], place_ref[3]

        @pl.when(step == 0)
        def _():
            total[...] = jnp.zeros_like(total)
            held = weight_transpose(cot_ref[...], up_ref[...]).astype(jnp.bfloat16)
            lgrad_ref[...] = held
            lgrad_t[...] = weight_transpose(up_ref[...], cot_ref[...]).astype(jnp.bfloat16)

        block = act_ref[...]
        total[...] += weight_transpose(block, down_ref[...])
        term = jnp.dot(lgrad_t[...], block, preferred_element_type=jnp.float32)
        z_of, y_of = step // 2, step % 2
        here = jnp.where(y_of == y, NZ, 0) + z_of
        at = pl.ds(pl.multiple_of(here * part, part), part)

        @pl.when(c == 0)
        def _():
            own_ref[:, at] = term[:, :part]
            away_ref[:, at] = term[:, part:]

        @pl.when(c == 1)
        def _():
            own_ref[:, at] = term[:, part:]
            away_ref[:, at] = term[:, :part]

        @pl.when(step == chips - 1)
        def _():
            latent = total[...].astype(jnp.bfloat16)
            latent_ref[...] = latent
            both = leading(latent, cot_ref[...])

            @pl.when(c == 0)
            def _():
                own_ref[:, chips * part :] = both[:, :up_part]
                away_ref[:, chips * part :] = both[:, up_part:]

            @pl.when(c == 1)
            def _():
                own_ref[:, chips * part :] = both[:, up_part:]
                away_ref[:, chips * part :] = both[:, :up_part]

    fixed = lambda shape: pl.BlockSpec(shape, lambda i: (0,) * len(shape))
    return pl.pallas_call(
        kernel,
        grid=(chips,),
        out_shape=[
            jax.ShapeDtypeStruct((tokens, rank), jnp.bfloat16),
            jax.ShapeDtypeStruct((tokens, rank), jnp.bfloat16),
            jax.ShapeDtypeStruct((rank, packed), jnp.float32),
            jax.ShapeDtypeStruct((rank, packed), jnp.float32),
        ],
        in_specs=[
            scalars(),
            pl.BlockSpec((tokens, chunk), lambda i: (0, i)),
            pl.BlockSpec((rank, chunk), lambda i: (0, i)),
            fixed((rank, features)),
            fixed((tokens, features)),
        ],
        out_specs=[
            fixed((tokens, rank)),
            fixed((tokens, rank)),
            fixed((rank, packed)),
            fixed((rank, packed)),
        ],
        scratch_shapes=[
            pltpu.VMEM((tokens, rank), jnp.float32),
            pltpu.VMEM((rank, tokens), jnp.bfloat16),
        ],
        compiler_params=params(),
        cost_estimate=LITTLE,
        name="local_gradients",
    )(place, activations, down_t, up, cotangent)


def add_cores(own, came, up_part):
    rank, packed = own.shape
    half = (packed - up_part) // 2

    def kernel(own_ref, came_ref, message_ref, kept_ref):
        message_ref[:, :half] = (own_ref[:, :half] + came_ref[:, :half]).astype(jnp.bfloat16)
        kept_ref[...] = own_ref[:, half : 2 * half] + came_ref[:, half : 2 * half]
        message_ref[:, half:] = (own_ref[:, 2 * half :] + came_ref[:, 2 * half :]).astype(
            jnp.bfloat16
        )

    return pl.pallas_call(
        kernel,
        out_shape=[
            jax.ShapeDtypeStruct((rank, half + up_part), jnp.bfloat16),
            jax.ShapeDtypeStruct((rank, half), jnp.float32),
        ],
        in_specs=[whole()] * 2,
        out_specs=[whole()] * 2,
        compiler_params=params(),
        cost_estimate=LITTLE,
        name="add_cores",
    )(own, came)


def add_y(place, kept, sent, came, up_part):
    rank, half = kept.shape
    part = half // NZ

    def kernel(place_ref, kept_ref, sent_ref, came_ref, up_ref, far_ref, down_ref, own_ref):
        z = place_ref[1]
        tail = sent_ref[:, half:].astype(jnp.float32) + came_ref[:, half:].astype(jnp.float32)
        tail = tail.astype(jnp.bfloat16)
        for shift, out_ref in ((0, own_ref), (1, up_ref), (2, far_ref), (3, down_ref)):
            at = pl.ds(pl.multiple_of(lax.rem(z + shift, NZ) * part, part), part)
            summed = kept_ref[:, at] + came_ref[:, at].astype(jnp.float32)
            out_ref[:, :part] = summed.astype(out_ref.dtype)
            out_ref[:, part:] = tail.astype(out_ref.dtype)

    shape = (rank, part + up_part)
    return pl.pallas_call(
        kernel,
        out_shape=[jax.ShapeDtypeStruct(shape, jnp.bfloat16)] * 3
        + [jax.ShapeDtypeStruct(shape, jnp.float32)],
        in_specs=[scalars()] + [whole()] * 3,
        out_specs=[whole()] * 4,
        compiler_params=params(),
        cost_estimate=LITTLE,
        name="add_y",
    )(place, kept, sent, came)


def add_z(own, from_down, from_far, from_up, up_part, factor):
    rank, wide = own.shape
    part = wide - up_part

    def kernel(own_ref, a_ref, b_ref, c_ref, gd_ref, gu_ref):
        f32 = jnp.float32
        summed = (own_ref[...] + b_ref[...].astype(f32)) + (
            a_ref[...].astype(f32) + c_ref[...].astype(f32)
        )
        summed = summed * factor
        gd_ref[...] = summed[:, :part]
        gu_ref[...] = summed[:, part:]

    return pl.pallas_call(
        kernel,
        out_shape=[
            jax.ShapeDtypeStruct((rank, part), jnp.float32),
            jax.ShapeDtypeStruct((rank, up_part), jnp.float32),
        ],
        in_specs=[whole()] * 4,
        out_specs=[whole()] * 2,
        compiler_params=params(),
        cost_estimate=LITTLE,
        name="add_z",
    )(own, from_down, from_far, from_up)


def join_cores(place, own, came):
    rank, up_part = own.shape

    def kernel(place_ref, own_ref, came_ref, out_ref):
        c = place_ref[3]
        out_ref[:, pl.ds(pl.multiple_of(c * up_part, up_part), up_part)] = own_ref[...]
        out_ref[:, pl.ds(pl.multiple_of((1 - c) * up_part, up_part), up_part)] = came_ref[...]

    return pl.pallas_call(
        kernel,
        out_shape=jax.ShapeDtypeStruct((rank, 2 * up_part), jnp.float32),
        in_specs=[scalars(), whole(), whole()],
        out_specs=whole(),
        compiler_params=params(),
        cost_estimate=LITTLE,
        name="join_cores",
    )(place, own, came)


def multiply(
    place, keys, pieces, activations, down_t, cotangent, lgrad, total, gradient, finish=None
):
    count = len(pieces)
    tokens, width = activations.shape
    rank = down_t.shape[0]
    rows, features = pieces[0].shape
    started = total is not None

    def kernel(*refs):
        refs = list(refs)
        place_ref, act_ref, down_ref, cot_ref, lgrad_ref = refs[:5]
        del refs[:5]
        if started:
            total_ref = refs.pop(0)
            refs.pop(0)
        if finish is not None:
            latent_ref, up_ref = refs.pop(0), refs.pop(0)
        piece_refs = refs[:count]
        del refs[:count]
        out_ref, grad_ref, weights, acts, downs, grads, in_sems, out_sems = refs
        g, z, y, c = (place_ref[i] for i in range(4))
        columns = []
        for dz, dy, dc, dh in keys:
            chip = lax.rem(z + (NZ - dz), NZ) * 2 + (1 - y if dy else y)
            device = chip * 2 + (1 - c if dc else c)
            start = (device * 2 + (1 - g if dh else g)) * rows
            columns.append(pl.ds(pl.multiple_of(start, rows), rows))
        coming, going = [], []
        for p in range(count):
            at = columns[p]
            trio = [
                pltpu.make_async_copy(piece_refs[p], weights.at[p], in_sems.at[3 * p]),
                pltpu.make_async_copy(act_ref.at[:, at], acts.at[p], in_sems.at[3 * p + 1]),
                pltpu.make_async_copy(down_ref.at[:, at], downs.at[p], in_sems.at[3 * p + 2]),
            ]
            for copy in trio:
                copy.start()
            coming.append(trio)
        if finish is not None:
            sum_so_far = total_ref[...] + lowrank_scale * jnp.dot(
                latent_ref[...], up_ref[...], preferred_element_type=jnp.float32
            )
        elif started:
            sum_so_far = total_ref[...]
        else:
            sum_so_far = None
        for p in range(count):
            for copy in coming[p]:
                copy.wait()
            weight = weights[p]
            term = jnp.dot(acts[p], weight, preferred_element_type=jnp.float32)
            sum_so_far = term if sum_so_far is None else sum_so_far + term
            grads[p] = (
                weight_transpose(cot_ref[...], weight)
                + lowrank_scale
                * jnp.dot(lgrad_ref[...], downs[p], preferred_element_type=jnp.float32)
            ).astype(jnp.bfloat16)
            copy = pltpu.make_async_copy(grads.at[p], grad_ref.at[:, columns[p]], out_sems.at[p])
            copy.start()
            going.append(copy)
        out_ref[...] = sum_so_far.astype(out_ref.dtype)
        for copy in going:
            copy.wait()

    operands = [place, activations, down_t, cotangent, lgrad]
    specs = [scalars(), anywhere(), anywhere(), whole(), whole()]
    aliases = {}
    if started:
        operands += [total, gradient]
        specs += [whole(), anywhere()]
        aliases = {6: 1}
    if finish is not None:
        operands += list(finish)
        specs += [whole(), whole()]
    operands += list(pieces)
    specs += [anywhere()] * count
    out_type = jnp.float32 if finish is None else jnp.bfloat16
    return pl.pallas_call(
        kernel,
        out_shape=[
            jax.ShapeDtypeStruct((tokens, features), out_type),
            jax.ShapeDtypeStruct((tokens, width), jnp.bfloat16),
        ],
        in_specs=specs,
        out_specs=[whole(), anywhere()],
        scratch_shapes=[
            pltpu.VMEM((count, rows, features), jnp.bfloat16),
            pltpu.VMEM((count, tokens, rows), jnp.bfloat16),
            pltpu.VMEM((count, rank, rows), jnp.bfloat16),
            pltpu.VMEM((count, tokens, rows), jnp.bfloat16),
            pltpu.SemaphoreType.DMA((3 * count,)),
            pltpu.SemaphoreType.DMA((count,)),
        ],
        input_output_aliases=aliases,
        compiler_params=params(),
        cost_estimate=LITTLE,
        name="multiply",
    )(*operands)


def per_device(
    activations, quant_codes, block_scales, lowrank_down_factor, lowrank_up_factor, cotangent
):
    g = lax.axis_index("groups")
    f = lax.axis_index("fsdp")
    c, y, z = f & 1, (f >> 1) & 1, f >> 2
    place = jnp.stack([g, z, y, c]).astype(jnp.int32)
    shard = quant_codes.shape[0]
    half = shard // 2
    up_part = lowrank_up_factor.shape[1] // 2
    down_t = lowrank_down_factor.T
    factor = lowrank_scale / math.sqrt(activations.shape[0] * lax.axis_size("fsdp"))

    def both_cores(keys):
        return [(a, b, 0, h) for a, b, h in keys] + [(a, b, 1, h) for a, b, h in keys]

    barrier = lax.optimization_barrier
    held = {}

    held[0, 0, 0], held[0, 0, 1] = dequantize_halves(place, quant_codes, block_scales)
    own_keys = [(0, 0, 0), (0, 0, 1)]

    r1 = {
        (1, 0, 0): send(held[0, 0, 0], Z_UP),
        (3, 0, 0): send(held[0, 0, 0], Z_DOWN),
        (0, 1, 0): send(held[0, 0, 0], OVER_Y),
        (0, 1, 1): send(held[0, 0, 1], OVER_Y),
    }
    swapped = [send(held[k], OVER_CORE) for k in own_keys]
    latent, lgrad, own_terms, away_terms = local_gradients(
        place, activations, down_t, lowrank_up_factor, cotangent
    )
    came = send(away_terms, OVER_CORE)
    total, gradient = multiply(
        place, both_cores(own_keys),
        [held[k] for k in own_keys] + swapped,
        activations, down_t, cotangent, lgrad, None, None,
    )
    message_y, kept = add_cores(own_terms, came, up_part)
    r1, message_y, kept, total, gradient = barrier((r1, message_y, kept, total, gradient))
    held.update(r1)

    r2 = {
        (1, 1, 0): send(held[1, 0, 0], OVER_Y),
        (1, 0, 1): send(held[1, 0, 0], OVER_X),
        (3, 0, 1): send(held[3, 0, 0], OVER_X),
        (2, 0, 0): send(held[1, 0, 0], Z_UP),
        (3, 1, 1): send(held[0, 1, 1], Z_DOWN),
    }
    came_y = send(message_y, OVER_Y)
    keys = list(r1)
    swapped = [send(held[k], OVER_CORE) for k in keys]
    total, gradient = multiply(
        place, both_cores(keys),
        [held[k] for k in keys] + swapped,
        activations, down_t, cotangent, lgrad, total, gradient,
    )
    r2, came_y, total, gradient = barrier((r2, came_y, total, gradient))
    held.update(r2)

    to_up, to_far, to_down, own_part = add_y(place, kept, message_y, came_y, up_part)
    r3 = {
        (3, 1, 0): send(held[3, 0, 0], OVER_Y),
        (2, 1, 0): send(held[2, 0, 0], OVER_Y),
        (2, 0, 1): send(held[2, 0, 0], OVER_X),
        (1, 1, 1): send(held[1, 1, 0], OVER_X),
        (2, 1, 1): send(held[3, 1, 1], Z_DOWN),
    }
    from_down, from_far, from_up = send(to_up, Z_UP), send(to_far, Z_FAR), send(to_down, Z_DOWN)
    keys = list(r2)
    swapped = [send(held[k], OVER_CORE) for k in keys]
    total, gradient = multiply(
        place, both_cores(keys),
        [held[k] for k in keys] + swapped,
        activations, down_t, cotangent, lgrad, total, gradient,
    )
    r3, from_down, from_far, from_up, total, gradient = barrier(
        (r3, from_down, from_far, from_up, total, gradient)
    )
    held.update(r3)

    keys = list(r3)
    swapped = [send(held[k], OVER_CORE) for k in keys]
    grad_down_t, up_own = add_z(own_part, from_down, from_far, from_up, up_part, factor)
    up_came = send(up_own, OVER_CORE)
    total, gradient = multiply(
        place, both_cores(keys)[: len(keys)], [held[k] for k in keys],
        activations, down_t, cotangent, lgrad, total, gradient,
    )
    projected, gradient = multiply(
        place, both_cores(keys)[len(keys) :], swapped,
        activations, down_t, cotangent, lgrad, total, gradient,
        finish=(latent, lowrank_up_factor),
    )
    grad_up = join_cores(place, up_own, up_came)
    return (projected, gradient, grad_down_t.T, grad_up)


def solution(mesh):
    in_specs = (
        P(("groups", "fsdp"), None),
        P("fsdp", None),
        P("fsdp", None),
        P("groups", None),
        P("groups", None),
        P(("groups", "fsdp"), None),
    )
    out_specs = (
        P(("groups", "fsdp"), None),
        P(("groups", "fsdp"), None),
        P(("groups", "fsdp"), None),
        P("groups", None),
    )
    small = mesh.shape["groups"] == 2 and mesh.shape["fsdp"] == NZ * 4
    return jax.shard_map(
        per_device if small else per_device_general,
        mesh=mesh,
        in_specs=in_specs,
        out_specs=out_specs,
        check_vma=False,
    )
```

```python
import math

import jax
import jax.numpy as jnp
from jax import lax
from jax.experimental import pallas as pl
from jax.experimental.pallas import tpu as pltpu
from jax.sharding import PartitionSpec as P

BLOCK = 128
AXES = ("groups", "fsdp")

lowrank_scale = 0.5


def weight_transpose(left, right):
    return lax.dot_general(
        left, right, (((1,), (1,)), ((), ())), preferred_element_type=jnp.float32
    )


def leading(left, right):
    return lax.dot_general(
        left, right, (((0,), (0,)), ((), ())), preferred_element_type=jnp.float32
    )


def dequantize(quant_codes, block_scales):
    spread_scales = jnp.repeat(jnp.repeat(block_scales, BLOCK, axis=0), BLOCK, axis=1)
    return (quant_codes.astype(jnp.float32) * spread_scales).astype(jnp.bfloat16)


def per_device_general(
    activations, quant_codes, block_scales, lowrank_down_factor, lowrank_up_factor, cotangent
):
    value_weight = dequantize(quant_codes, block_scales)
    lowrank_hidden = jnp.dot(
        activations, lowrank_down_factor, preferred_element_type=jnp.float32
    ).astype(jnp.bfloat16)
    lowrank_update = lowrank_scale * jnp.dot(
        lowrank_hidden, lowrank_up_factor, preferred_element_type=jnp.float32
    )
    hidden_gradient = weight_transpose(cotangent, lowrank_up_factor).astype(jnp.bfloat16)
    gathered = lax.all_gather(value_weight, "fsdp", axis=0, tiled=True)
    projected = (
        lowrank_update + jnp.dot(activations, gathered, preferred_element_type=jnp.float32)
    ).astype(jnp.bfloat16)
    input_gradient = (
        weight_transpose(cotangent, gathered)
        + lowrank_scale * weight_transpose(hidden_gradient, lowrank_down_factor)
    ).astype(jnp.bfloat16)
    scaling_factor = lowrank_scale / math.sqrt(activations.shape[0] * lax.axis_size("fsdp"))
    grad_down = lax.psum_scatter(
        scaling_factor * leading(activations, hidden_gradient),
        "fsdp",
        scatter_dimension=0,
        tiled=True,
    )
    grad_up = lax.psum(scaling_factor * leading(lowrank_hidden, cotangent), "fsdp")
    return (projected, input_gradient, grad_down, grad_up)


NZ = 4
VMEM_LIMIT = 40 * 1024 * 1024


def pairs_of(move):
    found = []
    for g in range(2):
        for z in range(NZ):
            for y in range(2):
                for c in range(2):
                    to = move(g, z, y, c)
                    found.append((index_of(g, z, y, c), index_of(*to)))
    return found


def index_of(g, z, y, c):
    return ((g * NZ + z) * 2 + y) * 2 + c


OVER_CORE = pairs_of(lambda g, z, y, c: (g, z, y, 1 - c))
OVER_Y = pairs_of(lambda g, z, y, c: (g, z, 1 - y, c))
OVER_X = pairs_of(lambda g, z, y, c: (1 - g, z, y, c))
Z_UP = pairs_of(lambda g, z, y, c: (g, (z + 1) % NZ, y, c))
Z_DOWN = pairs_of(lambda g, z, y, c: (g, (z - 1) % NZ, y, c))
Z_FAR = pairs_of(lambda g, z, y, c: (g, (z + 2) % NZ, y, c))


def send(array, pairs):
    return lax.ppermute(array, AXES, pairs)


def whole():
    return pl.BlockSpec(memory_space=pltpu.VMEM)


def scalars():
    return pl.BlockSpec(memory_space=pltpu.SMEM)


def anywhere():
    return pl.BlockSpec(memory_space=pl.ANY)


def params():
    return pltpu.CompilerParams(vmem_limit_bytes=VMEM_LIMIT)


LITTLE = pl.CostEstimate(flops=1, bytes_accessed=1, transcendentals=0)


def dequantize_shard(place, quant_codes, block_scales):
    rows, columns = quant_codes.shape
    half = rows // 2

    def kernel(place_ref, codes_ref, scales_ref, own_ref, first_ref):
        g = place_ref[0]
        for i in range(rows // BLOCK):
            source = lax.rem(g * (half // BLOCK) + i, rows // BLOCK)
            start = pl.multiple_of(source * BLOCK, BLOCK)
            for j in range(columns // BLOCK):
                at = slice(j * BLOCK, (j + 1) * BLOCK)
                block = codes_ref[pl.ds(start, BLOCK), at].astype(jnp.float32)
                block = (block * scales_ref[source, j]).astype(jnp.bfloat16)
                own_ref[i * BLOCK : (i + 1) * BLOCK, at] = block
                if i < half // BLOCK:
                    first_ref[i * BLOCK : (i + 1) * BLOCK, at] = block

    return pl.pallas_call(
        kernel,
        out_shape=[
            jax.ShapeDtypeStruct((rows, columns), jnp.bfloat16),
            jax.ShapeDtypeStruct((half, columns), jnp.bfloat16),
        ],
        in_specs=[scalars(), whole(), scalars()],
        out_specs=[whole()] * 2,
        compiler_params=params(),
        cost_estimate=LITTLE,
        name="dequantize",
    )(place, quant_codes, block_scales)


def local_gradients(place, activations, down_t, up, cotangent):
    tokens, width = activations.shape
    rank, features = up.shape
    chips = NZ * 2
    chunk = width // chips
    part = chunk // 2
    up_part = features // 2
    packed = chips * part + up_part

    def kernel(
        place_ref, act_ref, down_ref, up_ref, cot_ref, latent_ref, lgrad_ref, own_ref, away_ref,
        total, lgrad_t,
    ):
        step = pl.program_id(0)
        y, c = place_ref[2], place_ref[3]

        @pl.when(step == 0)
        def _():
            total[...] = jnp.zeros_like(total)
            held = weight_transpose(cot_ref[...], up_ref[...]).astype(jnp.bfloat16)
            lgrad_ref[...] = held
            lgrad_t[...] = weight_transpose(up_ref[...], cot_ref[...]).astype(jnp.bfloat16)

        block = act_ref[...]
        total[...] += weight_transpose(block, down_ref[...])
        term = jnp.dot(lgrad_t[...], block, preferred_element_type=jnp.float32)
        z_of, y_of = step // 2, step % 2
        here = jnp.where(y_of == y, NZ, 0) + z_of
        at = pl.ds(pl.multiple_of(here * part, part), part)

        @pl.when(c == 0)
        def _():
            own_ref[:, at] = term[:, :part]
            away_ref[:, at] = term[:, part:]

        @pl.when(c == 1)
        def _():
            own_ref[:, at] = term[:, part:]
            away_ref[:, at] = term[:, :part]

        @pl.when(step == chips - 1)
        def _():
            latent = total[...].astype(jnp.bfloat16)
            latent_ref[...] = latent
            both = leading(latent, cot_ref[...])

            @pl.when(c == 0)
            def _():
                own_ref[:, chips * part :] = both[:, :up_part]
                away_ref[:, chips * part :] = both[:, up_part:]

            @pl.when(c == 1)
            def _():
                own_ref[:, chips * part :] = both[:, up_part:]
                away_ref[:, chips * part :] = both[:, :up_part]

    fixed = lambda shape: pl.BlockSpec(shape, lambda i: (0,) * len(shape))
    return pl.pallas_call(
        kernel,
        grid=(chips,),
        out_shape=[
            jax.ShapeDtypeStruct((tokens, rank), jnp.bfloat16),
            jax.ShapeDtypeStruct((tokens, rank), jnp.bfloat16),
            jax.ShapeDtypeStruct((rank, packed), jnp.float32),
            jax.ShapeDtypeStruct((rank, packed), jnp.float32),
        ],
        in_specs=[
            scalars(),
            pl.BlockSpec((tokens, chunk), lambda i: (0, i)),
            pl.BlockSpec((rank, chunk), lambda i: (0, i)),
            fixed((rank, features)),
            fixed((tokens, features)),
        ],
        out_specs=[
            fixed((tokens, rank)),
            fixed((tokens, rank)),
            fixed((rank, packed)),
            fixed((rank, packed)),
        ],
        scratch_shapes=[
            pltpu.VMEM((tokens, rank), jnp.float32),
            pltpu.VMEM((rank, tokens), jnp.bfloat16),
        ],
        compiler_params=params(),
        cost_estimate=LITTLE,
        name="local_gradients",
    )(place, activations, down_t, up, cotangent)


def fold(array):
    rank = array.shape[0]
    return jnp.concatenate([array[: rank // 2], array[rank // 2 :]], axis=1)


def add_cores(own, came, up_part):
    rank, packed = own.shape
    part = (packed - up_part) // (2 * NZ)
    half = NZ * part

    def kernel(own_ref, came_ref, message_ref, kept_ref):
        for z in range(NZ):
            at = slice(z * part, (z + 1) * part)
            message_ref[z * rank : (z + 1) * rank, :] = (
                own_ref[:, at] + came_ref[:, at]
            ).astype(jnp.bfloat16)
        kept_ref[...] = own_ref[:, half : 2 * half] + came_ref[:, half : 2 * half]
        message_ref[NZ * rank :, :] = fold(
            own_ref[:, 2 * half :] + came_ref[:, 2 * half :]
        ).astype(jnp.bfloat16)

    return pl.pallas_call(
        kernel,
        out_shape=[
            jax.ShapeDtypeStruct((NZ * rank + rank // 2, part), jnp.bfloat16),
            jax.ShapeDtypeStruct((rank, half), jnp.float32),
        ],
        in_specs=[whole()] * 2,
        out_specs=[whole()] * 2,
        compiler_params=params(),
        cost_estimate=LITTLE,
        name="add_cores",
    )(own, came)


def add_y(place, kept, sent, came, came_from):
    rank, half = kept.shape
    part = half // NZ
    rows = rank + rank // 2

    def kernel(place_ref, kept_ref, sent_ref, came_ref, own_ref, up_ref, far_ref, down_ref):
        z = place_ref[1]
        tail = sent_ref[NZ * rank :, :].astype(jnp.float32) + came_ref[
            came_from + NZ * rank :, :
        ].astype(jnp.float32)
        for shift, out_ref in ((0, own_ref), (1, up_ref), (2, far_ref), (3, down_ref)):
            to = lax.rem(z + shift, NZ)
            kept_at = pl.ds(pl.multiple_of(to * part, part), part)
            came_at = pl.ds(pl.multiple_of(came_from + to * rank, rank), rank)
            summed = kept_ref[:, kept_at] + came_ref[came_at, :].astype(jnp.float32)
            out_ref[:rank, :] = summed.astype(out_ref.dtype)
            out_ref[rank:, :] = tail.astype(jnp.bfloat16).astype(out_ref.dtype)

    return pl.pallas_call(
        kernel,
        out_shape=[jax.ShapeDtypeStruct((rows, part), jnp.float32)]
        + [jax.ShapeDtypeStruct((rows, part), jnp.bfloat16)] * 3,
        in_specs=[scalars()] + [whole()] * 3,
        out_specs=[whole()] * 4,
        compiler_params=params(),
        cost_estimate=LITTLE,
        name="add_y",
    )(place, kept, sent, came)


def add_z(own, from_down, from_far, from_up, up_from, factor):
    rows, part = own.shape
    rank = rows * 2 // 3

    def kernel(own_ref, a_ref, b_ref, c_ref, gd_ref, gu_ref):
        f32 = jnp.float32
        summed = (own_ref[...] + b_ref[...].astype(f32)) + (
            a_ref[...].astype(f32) + c_ref[up_from : up_from + rows, :].astype(f32)
        )
        summed = summed * factor
        gd_ref[...] = summed[:rank, :]
        gu_ref[...] = summed[rank:, :]

    return pl.pallas_call(
        kernel,
        out_shape=[
            jax.ShapeDtypeStruct((rank, part), jnp.float32),
            jax.ShapeDtypeStruct((rows - rank, part), jnp.float32),
        ],
        in_specs=[whole()] * 4,
        out_specs=[whole()] * 2,
        compiler_params=params(),
        cost_estimate=LITTLE,
        name="add_z",
    )(own, from_down, from_far, from_up)


def join_cores(place, own, came):
    half, folded = own.shape
    width = folded // 2

    def kernel(place_ref, own_ref, came_ref, out_ref):
        c = place_ref[3]
        for ref, core in ((own_ref, c), (came_ref, 1 - c)):
            at = pl.ds(pl.multiple_of(core * width, width), width)
            out_ref[:half, at] = ref[:, :width]
            out_ref[half:, at] = ref[:, width:]

    return pl.pallas_call(
        kernel,
        out_shape=jax.ShapeDtypeStruct((2 * half, folded), jnp.float32),
        in_specs=[scalars(), whole(), whole()],
        out_specs=whole(),
        compiler_params=params(),
        cost_estimate=LITTLE,
        name="join_cores",
    )(place, own, came)


def multiply(place, pieces, activations, down_t, cotangent, lgrad, total, gradient, finish=None):
    tokens, width = activations.shape
    features = cotangent.shape[1]
    arrays = []
    for array, _, _ in pieces:
        if not any(array is other for other in arrays):
            arrays.append(array)
    where = [next(i for i, a in enumerate(arrays) if a is array) for array, _, _ in pieces]
    count = len(pieces)
    started = total is not None
    rows = width // (NZ * 2 * 2 * 2)

    def kernel(*refs):
        refs = list(refs)
        place_ref, act_ref, down_ref, cot_ref, lgrad_ref = refs[:5]
        del refs[:5]
        if started:
            total_ref = refs.pop(0)
            refs.pop(0)
        if finish is not None:
            latent_ref, up_ref = refs.pop(0), refs.pop(0)
        array_refs = refs[: len(arrays)]
        del refs[: len(arrays)]
        out_ref, grad_ref, sums, grads, out_sems = refs
        g, z, y, c = (place_ref[i] for i in range(4))
        if finish is not None:
            sums[...] = total_ref[...] + lowrank_scale * jnp.dot(
                latent_ref[...], up_ref[...], preferred_element_type=jnp.float32
            )
        elif started:
            sums[...] = total_ref[...]
        else:
            sums[...] = jnp.zeros_like(sums)
        going = []
        for p, (_, first, (dz, dy, dc, dh)) in enumerate(pieces):
            chip = lax.rem(z + (NZ - dz), NZ) * 2 + (1 - y if dy else y)
            device = chip * 2 + (1 - c if dc else c)
            start = (device * 2 + (1 - g if dh else g)) * rows
            at = pl.ds(pl.multiple_of(start, rows), rows)
            weight = array_refs[where[p]][first : first + rows, :]
            sums[...] += jnp.dot(act_ref[:, at], weight, preferred_element_type=jnp.float32)
            grads[p] = (
                weight_transpose(cot_ref[...], weight)
                + lowrank_scale
                * jnp.dot(lgrad_ref[...], down_ref[:, at], preferred_element_type=jnp.float32)
            ).astype(jnp.bfloat16)
            copy = pltpu.make_async_copy(grads.at[p], grad_ref.at[:, at], out_sems.at[p])
            copy.start()
            going.append(copy)
        out_ref[...] = sums[...].astype(out_ref.dtype)
        for copy in going:
            copy.wait()

    operands = [place, activations, down_t, cotangent, lgrad]
    specs = [scalars()] + [whole()] * 4
    aliases = {}
    if started:
        operands += [total, gradient]
        specs += [whole(), anywhere()]
        aliases = {6: 1}
    if finish is not None:
        operands += list(finish)
        specs += [whole(), whole()]
    operands += arrays
    specs += [whole()] * len(arrays)
    out_type = jnp.float32 if finish is None else jnp.bfloat16
    return pl.pallas_call(
        kernel,
        out_shape=[
            jax.ShapeDtypeStruct((tokens, features), out_type),
            jax.ShapeDtypeStruct((tokens, width), jnp.bfloat16),
        ],
        in_specs=specs,
        out_specs=[whole(), anywhere()],
        scratch_shapes=[
            pltpu.VMEM((tokens, features), jnp.float32),
            pltpu.VMEM((count, tokens, rows), jnp.bfloat16),
            pltpu.SemaphoreType.DMA((count,)),
        ],
        input_output_aliases=aliases,
        compiler_params=params(),
        cost_estimate=LITTLE,
        name="multiply",
    )(*operands)


def per_device(
    activations, quant_codes, block_scales, lowrank_down_factor, lowrank_up_factor, cotangent
):
    g = lax.axis_index("groups")
    f = lax.axis_index("fsdp")
    place = jnp.stack([g, f >> 2, (f >> 1) & 1, f & 1]).astype(jnp.int32)
    half = quant_codes.shape[0] // 2
    up_part = lowrank_up_factor.shape[1] // 2
    down_t = lowrank_down_factor.T
    factor = lowrank_scale / math.sqrt(activations.shape[0] * lax.axis_size("fsdp"))
    barrier = lax.optimization_barrier
    join = lambda *arrays: jnp.concatenate(arrays, axis=0)

    def products(pieces, total, gradient, finish=None):
        return multiply(
            place, pieces, activations, down_t, cotangent, lgrad, total, gradient, finish
        )

    def listed(array, dc, *keys):
        return [(array, i * half, (dz, dy, dc, dh)) for i, (dz, dy, dh) in enumerate(keys)]

    own, first = dequantize_shard(place, quant_codes, block_scales)
    own, first, place = barrier((own, first, place))

    y1, up1, down1 = send(own, OVER_Y), send(first, Z_UP), send(first, Z_DOWN)
    swap1 = send(own, OVER_CORE)
    latent, lgrad, own_terms, away_terms = local_gradients(
        place, activations, down_t, lowrank_up_factor, cotangent
    )
    came = send(away_terms, OVER_CORE)
    own_keys = [(0, 0, 0), (0, 0, 1)]
    total, gradient = products(
        listed(own, 0, *own_keys) + listed(swap1, 1, *own_keys), None, None
    )
    terms_y, kept = add_cores(own_terms, came, up_part)
    y1, up1, down1, terms_y, kept, total, gradient = barrier(
        (y1, up1, down1, terms_y, kept, total, gradient)
    )

    y2, x2 = send(join(up1, terms_y), OVER_Y), send(join(up1, down1), OVER_X)
    up2, down2 = send(up1, Z_UP), send(y1[half:], Z_DOWN)
    swap2 = send(join(up1, down1, y1), OVER_CORE)
    keys = [(1, 0, 0), (3, 0, 0), (0, 1, 0), (0, 1, 1)]
    total, gradient = products(
        listed(up1, 0, keys[0])
        + listed(down1, 0, keys[1])
        + listed(y1, 0, *keys[2:])
        + listed(swap2, 1, *keys),
        total, gradient,
    )
    y2, x2, up2, down2, total, gradient = barrier((y2, x2, up2, down2, total, gradient))

    own_part, to_up, to_far, to_down = add_y(place, kept, terms_y, y2, half)
    y3, x3 = send(join(down1, up2), OVER_Y), send(join(up2, y2[:half]), OVER_X)
    down3, up3 = send(join(down2, to_down), Z_DOWN), send(to_up, Z_UP)
    swap3 = send(join(y2[:half], x2, up2, down2), OVER_CORE)
    swap3, to_far = barrier((swap3, to_far))
    far3 = send(to_far, Z_FAR)
    keys = [(1, 1, 0), (1, 0, 1), (3, 0, 1), (2, 0, 0), (3, 1, 1)]
    total, gradient = products(
        listed(y2, 0, keys[0])
        + listed(x2, 0, *keys[1:3])
        + listed(up2, 0, keys[3])
        + listed(down2, 0, keys[4])
        + listed(swap3, 1, *keys),
        total, gradient,
    )
    y3, x3, down3, up3, far3, total, gradient = barrier(
        (y3, x3, down3, up3, far3, total, gradient)
    )

    swap4 = send(join(y3, x3, down3[:half]), OVER_CORE)
    grad_down_t, up_own = add_z(own_part, up3, far3, down3, half, factor)
    up_came = send(up_own, OVER_CORE)
    keys = [(3, 1, 0), (2, 1, 0), (2, 0, 1), (1, 1, 1), (2, 1, 1)]
    total, gradient = products(
        listed(y3, 0, *keys[:2]) + listed(x3, 0, *keys[2:4]) + listed(down3, 0, keys[4]),
        total, gradient,
    )
    projected, gradient = products(
        listed(swap4, 1, *keys), total, gradient, finish=(latent, lowrank_up_factor)
    )
    grad_up = join_cores(place, up_own, up_came)
    return (projected, gradient, grad_down_t.T, grad_up)


def solution(mesh):
    in_specs = (
        P(("groups", "fsdp"), None),
        P("fsdp", None),
        P("fsdp", None),
        P("groups", None),
        P("groups", None),
        P(("groups", "fsdp"), None),
    )
    out_specs = (
        P(("groups", "fsdp"), None),
        P(("groups", "fsdp"), None),
        P(("groups", "fsdp"), None),
        P("groups", None),
    )
    small = mesh.shape["groups"] == 2 and mesh.shape["fsdp"] == NZ * 4
    return jax.shard_map(
        per_device if small else per_device_general,
        mesh=mesh,
        in_specs=in_specs,
        out_specs=out_specs,
        check_vma=False,
    )
```

```python
import math

import jax
import jax.numpy as jnp
from jax import lax
from jax.experimental import pallas as pl
from jax.experimental.pallas import tpu as pltpu
from jax.sharding import PartitionSpec as P

BLOCK = 128
AXES = ("groups", "fsdp")

lowrank_scale = 0.5


def weight_transpose(left, right):
    return lax.dot_general(
        left, right, (((1,), (1,)), ((), ())), preferred_element_type=jnp.float32
    )


def leading(left, right):
    return lax.dot_general(
        left, right, (((0,), (0,)), ((), ())), preferred_element_type=jnp.float32
    )


def dequantize(quant_codes, block_scales):
    spread_scales = jnp.repeat(jnp.repeat(block_scales, BLOCK, axis=0), BLOCK, axis=1)
    return (quant_codes.astype(jnp.float32) * spread_scales).astype(jnp.bfloat16)


def per_device_general(
    activations, quant_codes, block_scales, lowrank_down_factor, lowrank_up_factor, cotangent
):
    value_weight = dequantize(quant_codes, block_scales)
    lowrank_hidden = jnp.dot(
        activations, lowrank_down_factor, preferred_element_type=jnp.float32
    ).astype(jnp.bfloat16)
    lowrank_update = lowrank_scale * jnp.dot(
        lowrank_hidden, lowrank_up_factor, preferred_element_type=jnp.float32
    )
    hidden_gradient = weight_transpose(cotangent, lowrank_up_factor).astype(jnp.bfloat16)
    gathered = lax.all_gather(value_weight, "fsdp", axis=0, tiled=True)
    projected = (
        lowrank_update + jnp.dot(activations, gathered, preferred_element_type=jnp.float32)
    ).astype(jnp.bfloat16)
    input_gradient = (
        weight_transpose(cotangent, gathered)
        + lowrank_scale * weight_transpose(hidden_gradient, lowrank_down_factor)
    ).astype(jnp.bfloat16)
    scaling_factor = lowrank_scale / math.sqrt(activations.shape[0] * lax.axis_size("fsdp"))
    grad_down = lax.psum_scatter(
        scaling_factor * leading(activations, hidden_gradient),
        "fsdp",
        scatter_dimension=0,
        tiled=True,
    )
    grad_up = lax.psum(scaling_factor * leading(lowrank_hidden, cotangent), "fsdp")
    return (projected, input_gradient, grad_down, grad_up)


NZ = 4
VMEM_LIMIT = 40 * 1024 * 1024


def pairs_of(move):
    found = []
    for g in range(2):
        for z in range(NZ):
            for y in range(2):
                for c in range(2):
                    to = move(g, z, y, c)
                    found.append((index_of(g, z, y, c), index_of(*to)))
    return found


def index_of(g, z, y, c):
    return ((g * NZ + z) * 2 + y) * 2 + c


OVER_CORE = pairs_of(lambda g, z, y, c: (g, z, y, 1 - c))
OVER_Y = pairs_of(lambda g, z, y, c: (g, z, 1 - y, c))
OVER_X = pairs_of(lambda g, z, y, c: (1 - g, z, y, c))
Z_UP = pairs_of(lambda g, z, y, c: (g, (z + 1) % NZ, y, c))
Z_DOWN = pairs_of(lambda g, z, y, c: (g, (z - 1) % NZ, y, c))
Z_FAR = pairs_of(lambda g, z, y, c: (g, (z + 2) % NZ, y, c))


def send(array, pairs):
    return lax.ppermute(array, AXES, pairs)


def whole():
    return pl.BlockSpec(memory_space=pltpu.VMEM)


def scalars():
    return pl.BlockSpec(memory_space=pltpu.SMEM)


def in_hbm():
    return pl.BlockSpec(memory_space=pltpu.HBM)


def params():
    return pltpu.CompilerParams(vmem_limit_bytes=VMEM_LIMIT)


LITTLE = pl.CostEstimate(flops=1, bytes_accessed=1, transcendentals=0)


def dequantize_shard(place, quant_codes, block_scales):
    rows, columns = quant_codes.shape
    half = rows // 2

    def kernel(place_ref, codes_hbm, scales_hbm, own_ref, first_ref, codes_ref, scales_ref, sems):
        copies = [
            pltpu.make_async_copy(scales_hbm, scales_ref, sems.at[0]),
            pltpu.make_async_copy(codes_hbm, codes_ref, sems.at[1]),
        ]
        for copy in copies:
            copy.start()
        for copy in copies:
            copy.wait()
        g = place_ref[0]
        for i in range(rows // BLOCK):
            source = lax.rem(g * (half // BLOCK) + i, rows // BLOCK)
            start = pl.multiple_of(source * BLOCK, BLOCK)
            for j in range(columns // BLOCK):
                at = slice(j * BLOCK, (j + 1) * BLOCK)
                block = codes_ref[pl.ds(start, BLOCK), at].astype(jnp.float32)
                block = (block * scales_ref[source, j]).astype(jnp.bfloat16)
                own_ref[i * BLOCK : (i + 1) * BLOCK, at] = block
                if i < half // BLOCK:
                    first_ref[i * BLOCK : (i + 1) * BLOCK, at] = block

    return pl.pallas_call(
        kernel,
        out_shape=[
            jax.ShapeDtypeStruct((rows, columns), jnp.bfloat16),
            jax.ShapeDtypeStruct((half, columns), jnp.bfloat16),
        ],
        in_specs=[scalars(), in_hbm(), in_hbm()],
        out_specs=[whole()] * 2,
        scratch_shapes=[
            pltpu.VMEM(quant_codes.shape, quant_codes.dtype),
            pltpu.SMEM(block_scales.shape, block_scales.dtype),
            pltpu.SemaphoreType.DMA((2,)),
        ],
        compiler_params=params(),
        cost_estimate=LITTLE,
        name="dequantize",
    )(place, quant_codes, block_scales)


def local_gradients(place, activations, down_t, up, cotangent):
    tokens, width = activations.shape
    rank, features = up.shape
    chips = NZ * 2
    chunk = width // chips
    part = chunk // 2
    up_part = features // 2
    packed = chips * part + up_part

    def kernel(
        place_ref, act_ref, down_ref, up_ref, cot_ref, latent_ref, lgrad_ref, own_ref, away_ref,
        total, lgrad_t,
    ):
        step = pl.program_id(0)
        y, c = place_ref[2], place_ref[3]

        @pl.when(step == 0)
        def _():
            total[...] = jnp.zeros_like(total)
            held = weight_transpose(cot_ref[...], up_ref[...]).astype(jnp.bfloat16)
            lgrad_ref[...] = held
            lgrad_t[...] = weight_transpose(up_ref[...], cot_ref[...]).astype(jnp.bfloat16)

        block = act_ref[...]
        total[...] += weight_transpose(block, down_ref[...])
        term = jnp.dot(lgrad_t[...], block, preferred_element_type=jnp.float32)
        z_of, y_of = step // 2, step % 2
        here = jnp.where(y_of == y, NZ, 0) + z_of
        at = pl.ds(pl.multiple_of(here * part, part), part)

        @pl.when(c == 0)
        def _():
            own_ref[:, at] = term[:, :part]
            away_ref[:, at] = term[:, part:]

        @pl.when(c == 1)
        def _():
            own_ref[:, at] = term[:, part:]
            away_ref[:, at] = term[:, :part]

        @pl.when(step == chips - 1)
        def _():
            latent = total[...].astype(jnp.bfloat16)
            latent_ref[...] = latent
            both = leading(latent, cot_ref[...])

            @pl.when(c == 0)
            def _():
                own_ref[:, chips * part :] = both[:, :up_part]
                away_ref[:, chips * part :] = both[:, up_part:]

            @pl.when(c == 1)
            def _():
                own_ref[:, chips * part :] = both[:, up_part:]
                away_ref[:, chips * part :] = both[:, :up_part]

    fixed = lambda shape: pl.BlockSpec(shape, lambda i: (0,) * len(shape))
    return pl.pallas_call(
        kernel,
        grid=(chips,),
        out_shape=[
            jax.ShapeDtypeStruct((tokens, rank), jnp.bfloat16),
            jax.ShapeDtypeStruct((tokens, rank), jnp.bfloat16),
            jax.ShapeDtypeStruct((rank, packed), jnp.float32),
            jax.ShapeDtypeStruct((rank, packed), jnp.float32),
        ],
        in_specs=[
            scalars(),
            pl.BlockSpec((tokens, chunk), lambda i: (0, i)),
            pl.BlockSpec((rank, chunk), lambda i: (0, i)),
            fixed((rank, features)),
            fixed((tokens, features)),
        ],
        out_specs=[
            fixed((tokens, rank)),
            fixed((tokens, rank)),
            fixed((rank, packed)),
            fixed((rank, packed)),
        ],
        scratch_shapes=[
            pltpu.VMEM((tokens, rank), jnp.float32),
            pltpu.VMEM((rank, tokens), jnp.bfloat16),
        ],
        compiler_params=params(),
        cost_estimate=LITTLE,
        name="local_gradients",
    )(place, activations, down_t, up, cotangent)


def fold(array):
    rank = array.shape[0]
    return jnp.concatenate([array[: rank // 2], array[rank // 2 :]], axis=1)


def add_cores(own, came, up_part):
    rank, packed = own.shape
    part = (packed - up_part) // (2 * NZ)
    half = NZ * part

    def kernel(own_ref, came_ref, message_ref, kept_ref):
        for z in range(NZ):
            at = slice(z * part, (z + 1) * part)
            message_ref[z * rank : (z + 1) * rank, :] = (
                own_ref[:, at] + came_ref[:, at]
            ).astype(jnp.bfloat16)
        kept_ref[...] = own_ref[:, half : 2 * half] + came_ref[:, half : 2 * half]
        message_ref[NZ * rank :, :] = fold(
            own_ref[:, 2 * half :] + came_ref[:, 2 * half :]
        ).astype(jnp.bfloat16)

    return pl.pallas_call(
        kernel,
        out_shape=[
            jax.ShapeDtypeStruct((NZ * rank + rank // 2, part), jnp.bfloat16),
            jax.ShapeDtypeStruct((rank, half), jnp.float32),
        ],
        in_specs=[whole()] * 2,
        out_specs=[whole()] * 2,
        compiler_params=params(),
        cost_estimate=LITTLE,
        name="add_cores",
    )(own, came)


def add_y(place, kept, sent, came, came_from):
    rank, half = kept.shape
    part = half // NZ
    rows = rank + rank // 2

    def kernel(place_ref, kept_ref, sent_ref, came_ref, own_ref, up_ref, far_ref, down_ref):
        z = place_ref[1]
        tail = sent_ref[NZ * rank :, :].astype(jnp.float32) + came_ref[
            came_from + NZ * rank :, :
        ].astype(jnp.float32)
        for shift, out_ref in ((0, own_ref), (1, up_ref), (2, far_ref), (3, down_ref)):
            to = lax.rem(z + shift, NZ)
            kept_at = pl.ds(pl.multiple_of(to * part, part), part)
            came_at = pl.ds(pl.multiple_of(came_from + to * rank, rank), rank)
            summed = kept_ref[:, kept_at] + came_ref[came_at, :].astype(jnp.float32)
            out_ref[:rank, :] = summed.astype(out_ref.dtype)
            out_ref[rank:, :] = tail.astype(jnp.bfloat16).astype(out_ref.dtype)

    return pl.pallas_call(
        kernel,
        out_shape=[jax.ShapeDtypeStruct((rows, part), jnp.float32)]
        + [jax.ShapeDtypeStruct((rows, part), jnp.bfloat16)] * 3,
        in_specs=[scalars()] + [whole()] * 3,
        out_specs=[whole()] * 4,
        compiler_params=params(),
        cost_estimate=LITTLE,
        name="add_y",
    )(place, kept, sent, came)


def add_z(own, from_down, from_far, from_up, up_from, factor):
    rows, part = own.shape
    rank = rows * 2 // 3

    def kernel(own_ref, a_ref, b_ref, c_ref, gd_ref, gu_ref):
        f32 = jnp.float32
        summed = (own_ref[...] + b_ref[...].astype(f32)) + (
            a_ref[...].astype(f32) + c_ref[up_from : up_from + rows, :].astype(f32)
        )
        summed = summed * factor
        gd_ref[...] = summed[:rank, :]
        gu_ref[...] = summed[rank:, :]

    return pl.pallas_call(
        kernel,
        out_shape=[
            jax.ShapeDtypeStruct((rank, part), jnp.float32),
            jax.ShapeDtypeStruct((rows - rank, part), jnp.float32),
        ],
        in_specs=[whole()] * 4,
        out_specs=[whole()] * 2,
        compiler_params=params(),
        cost_estimate=LITTLE,
        name="add_z",
    )(own, from_down, from_far, from_up)


def multiply(
    place, pieces, activations, down_t, cotangent, lgrad, begin=None, so_far=None, end=None
):
    tokens, width = activations.shape
    features = cotangent.shape[1]
    arrays = []
    for array, _, _ in pieces:
        if not any(array is other for other in arrays):
            arrays.append(array)
    where = [next(i for i, a in enumerate(arrays) if a is array) for array, _, _ in pieces]
    count = len(pieces)
    rows = width // (NZ * 2 * 2 * 2)

    def kernel(*refs):
        refs = list(refs)
        place_ref, act_ref, down_ref, cot_ref, lgrad_ref, one_ref, two_ref = refs[:7]
        del refs[:7]
        if end is not None:
            up_refs = refs[:2]
            del refs[:2]
        array_refs = refs[: len(arrays)]
        del refs[: len(arrays)]
        out_ref, grad_ref = refs[:2]
        sums, grads, out_sems = refs[-3:]
        g, z, y, c = (place_ref[i] for i in range(4))
        columns, weights, going = [], [], []
        for p, (_, first, (dz, dy, dc, dh)) in enumerate(pieces):
            chip = lax.rem(z + (NZ - dz), NZ) * 2 + (1 - y if dy else y)
            device = chip * 2 + (1 - c if dc else c)
            start = (device * 2 + (1 - g if dh else g)) * rows
            columns.append(pl.ds(pl.multiple_of(start, rows), rows))
            weights.append(array_refs[where[p]].at[first : first + rows, :])
        for p in range(count):
            grads[p] = (
                weight_transpose(cot_ref[...], weights[p][...])
                + lowrank_scale
                * jnp.dot(
                    lgrad_ref[...], down_ref[:, columns[p]], preferred_element_type=jnp.float32
                )
            ).astype(jnp.bfloat16)
            copy = pltpu.make_async_copy(grads.at[p], grad_ref.at[:, columns[p]], out_sems.at[p])
            copy.start()
            going.append(copy)
        if begin is not None:
            sums[...] = lowrank_scale * jnp.dot(
                one_ref[...], two_ref[...], preferred_element_type=jnp.float32
            )
        else:
            sums[...] = one_ref[...]
        for p in range(count):
            sums[...] += jnp.dot(
                act_ref[:, columns[p]], weights[p][...], preferred_element_type=jnp.float32
            )
        out_ref[...] = sums[...].astype(out_ref.dtype)
        if end is not None:
            up_part = features // 2
            rank = down_ref.shape[0]
            for ref, core in zip(up_refs, (c, 1 - c), strict=True):
                at = pl.ds(pl.multiple_of(core * up_part, up_part), up_part)
                refs[2][: rank // 2, at] = ref[:, :up_part]
                refs[2][rank // 2 :, at] = ref[:, up_part:]
        for copy in going:
            copy.wait()

    operands = [place, activations, down_t, cotangent, lgrad]
    specs = [scalars()] + [whole()] * 4
    out_shape = [
        jax.ShapeDtypeStruct((tokens, features), jnp.float32 if end is None else jnp.bfloat16),
        jax.ShapeDtypeStruct((tokens, width), jnp.bfloat16),
    ]
    out_specs = [whole(), in_hbm()]
    aliases = {}
    if begin is not None:
        operands += begin
        specs += [whole()] * 2
    else:
        operands += so_far
        specs += [whole(), in_hbm()]
        aliases = {6: 1}
    if end is not None:
        operands += end
        specs += [whole()] * 2
        out_shape.append(jax.ShapeDtypeStruct((down_t.shape[0], features), jnp.float32))
        out_specs.append(whole())
    return pl.pallas_call(
        kernel,
        out_shape=out_shape,
        in_specs=specs + [whole()] * len(arrays),
        out_specs=out_specs,
        scratch_shapes=[
            pltpu.VMEM((tokens, features), jnp.float32),
            pltpu.VMEM((count, tokens, rows), jnp.bfloat16),
            pltpu.SemaphoreType.DMA((count,)),
        ],
        input_output_aliases=aliases,
        compiler_params=params(),
        cost_estimate=LITTLE,
        name="multiply",
    )(*operands, *arrays)


def per_device(
    activations, quant_codes, block_scales, lowrank_down_factor, lowrank_up_factor, cotangent
):
    g = lax.axis_index("groups")
    f = lax.axis_index("fsdp")
    place = jnp.stack([g, f >> 2, (f >> 1) & 1, f & 1]).astype(jnp.int32)
    half = quant_codes.shape[0] // 2
    up_part = lowrank_up_factor.shape[1] // 2
    down_t = lowrank_down_factor.T
    factor = lowrank_scale / math.sqrt(activations.shape[0] * lax.axis_size("fsdp"))
    barrier = lax.optimization_barrier
    join = lambda *arrays: jnp.concatenate(arrays, axis=0)

    def products(pieces, **more):
        return multiply(place, pieces, activations, down_t, cotangent, lgrad, **more)

    def listed(array, dc, *keys):
        return [(array, i * half, (dz, dy, dc, dh)) for i, (dz, dy, dh) in enumerate(keys)]

    def block(body, *operands):
        def never(*operands):
            shapes = jax.eval_shape(body, *operands)
            return jax.tree.map(lambda shape: jnp.zeros(shape.shape, shape.dtype), shapes)

        return lax.cond(place[0] >= 0, body, never, *operands)

    own, first = dequantize_shard(place, quant_codes, block_scales)
    own, first, place = barrier((own, first, place))

    y1, up1, down1 = send(own, OVER_Y), send(first, Z_UP), send(first, Z_DOWN)
    swap1 = send(own, OVER_CORE)

    def lowrank(place):
        latent, lgrad, own_terms, away_terms = local_gradients(
            place, activations, down_t, lowrank_up_factor, cotangent
        )
        came = send(away_terms, OVER_CORE)
        terms_y, kept = add_cores(own_terms, came, up_part)
        return latent, lgrad, terms_y, kept

    latent, lgrad, terms_y, kept = block(lowrank, place)
    keys = [(0, 0, 0), (0, 0, 1)]
    done = products(
        listed(own, 0, *keys) + listed(swap1, 1, *keys), begin=[latent, lowrank_up_factor]
    )
    y1, up1, down1, terms_y, kept, done = barrier((y1, up1, down1, terms_y, kept, done))

    y2, x2 = send(join(up1, terms_y), OVER_Y), send(join(up1, down1), OVER_X)
    up2, down2 = send(up1, Z_UP), send(y1[half:], Z_DOWN)
    swap2 = send(join(up1, down1, y1), OVER_CORE)
    keys = [(1, 0, 0), (3, 0, 0), (0, 1, 0), (0, 1, 1)]
    done = products(
        listed(up1, 0, keys[0])
        + listed(down1, 0, keys[1])
        + listed(y1, 0, *keys[2:])
        + listed(swap2, 1, *keys),
        so_far=done,
    )
    y2, x2, up2, down2, done = barrier((y2, x2, up2, down2, done))

    own_part, to_up, to_far, to_down = add_y(place, kept, terms_y, y2, half)
    y3, x3 = send(join(down1, up2), OVER_Y), send(join(up2, y2[:half]), OVER_X)
    down3, up3 = send(join(down2, to_down), Z_DOWN), send(to_up, Z_UP)
    swap3 = send(join(y2[:half], x2, up2, down2), OVER_CORE)
    swap3, to_far = barrier((swap3, to_far))
    far3 = send(to_far, Z_FAR)
    keys = [(1, 1, 0), (1, 0, 1), (3, 0, 1), (2, 0, 0), (3, 1, 1)]
    done = products(
        listed(y2, 0, keys[0])
        + listed(x2, 0, *keys[1:3])
        + listed(up2, 0, keys[3])
        + listed(down2, 0, keys[4])
        + listed(swap3, 1, *keys),
        so_far=done,
    )
    y3, x3, down3, up3, far3, done = barrier((y3, x3, down3, up3, far3, done))

    swap4 = send(join(y3, x3, down3[:half]), OVER_CORE)
    grad_down_t, up_own = add_z(own_part, up3, far3, down3, half, factor)
    up_came = send(up_own, OVER_CORE)
    keys = [(3, 1, 0), (2, 1, 0), (2, 0, 1), (1, 1, 1), (2, 1, 1)]
    done = products(
        listed(y3, 0, *keys[:2]) + listed(x3, 0, *keys[2:4]) + listed(down3, 0, keys[4]),
        so_far=done,
    )
    projected, gradient, grad_up = products(
        listed(swap4, 1, *keys), so_far=done, end=[up_own, up_came]
    )
    return (projected, gradient, grad_down_t.T, grad_up)


def solution(mesh):
    in_specs = (
        P(("groups", "fsdp"), None),
        P("fsdp", None),
        P("fsdp", None),
        P("groups", None),
        P("groups", None),
        P(("groups", "fsdp"), None),
    )
    out_specs = (
        P(("groups", "fsdp"), None),
        P(("groups", "fsdp"), None),
        P(("groups", "fsdp"), None),
        P("groups", None),
    )
    small = mesh.shape["groups"] == 2 and mesh.shape["fsdp"] == NZ * 4
    return jax.shard_map(
        per_device if small else per_device_general,
        mesh=mesh,
        in_specs=in_specs,
        out_specs=out_specs,
        check_vma=False,
    )
```

```python
import math

import jax
import jax.numpy as jnp
from jax import lax
from jax.experimental import pallas as pl
from jax.experimental.pallas import tpu as pltpu
from jax.sharding import PartitionSpec as P

BLOCK = 128
AXES = ("groups", "fsdp")

lowrank_scale = 0.5


def weight_transpose(left, right):
    return lax.dot_general(
        left, right, (((1,), (1,)), ((), ())), preferred_element_type=jnp.float32
    )


def leading(left, right):
    return lax.dot_general(
        left, right, (((0,), (0,)), ((), ())), preferred_element_type=jnp.float32
    )


def dequantize(quant_codes, block_scales):
    spread_scales = jnp.repeat(jnp.repeat(block_scales, BLOCK, axis=0), BLOCK, axis=1)
    return (quant_codes.astype(jnp.float32) * spread_scales).astype(jnp.bfloat16)


def per_device_general(
    activations, quant_codes, block_scales, lowrank_down_factor, lowrank_up_factor, cotangent
):
    value_weight = dequantize(quant_codes, block_scales)
    lowrank_hidden = jnp.dot(
        activations, lowrank_down_factor, preferred_element_type=jnp.float32
    ).astype(jnp.bfloat16)
    lowrank_update = lowrank_scale * jnp.dot(
        lowrank_hidden, lowrank_up_factor, preferred_element_type=jnp.float32
    )
    hidden_gradient = weight_transpose(cotangent, lowrank_up_factor).astype(jnp.bfloat16)
    gathered = lax.all_gather(value_weight, "fsdp", axis=0, tiled=True)
    projected = (
        lowrank_update + jnp.dot(activations, gathered, preferred_element_type=jnp.float32)
    ).astype(jnp.bfloat16)
    input_gradient = (
        weight_transpose(cotangent, gathered)
        + lowrank_scale * weight_transpose(hidden_gradient, lowrank_down_factor)
    ).astype(jnp.bfloat16)
    scaling_factor = lowrank_scale / math.sqrt(activations.shape[0] * lax.axis_size("fsdp"))
    grad_down = lax.psum_scatter(
        scaling_factor * leading(activations, hidden_gradient),
        "fsdp",
        scatter_dimension=0,
        tiled=True,
    )
    grad_up = lax.psum(scaling_factor * leading(lowrank_hidden, cotangent), "fsdp")
    return (projected, input_gradient, grad_down, grad_up)


NZ = 4
VMEM_LIMIT = 40 * 1024 * 1024


def pairs_of(move):
    found = []
    for g in range(2):
        for z in range(NZ):
            for y in range(2):
                for c in range(2):
                    to = move(g, z, y, c)
                    found.append((index_of(g, z, y, c), index_of(*to)))
    return found


def index_of(g, z, y, c):
    return ((g * NZ + z) * 2 + y) * 2 + c


OVER_CORE = pairs_of(lambda g, z, y, c: (g, z, y, 1 - c))
OVER_Y = pairs_of(lambda g, z, y, c: (g, z, 1 - y, c))
OVER_X = pairs_of(lambda g, z, y, c: (1 - g, z, y, c))
Z_UP = pairs_of(lambda g, z, y, c: (g, (z + 1) % NZ, y, c))
Z_DOWN = pairs_of(lambda g, z, y, c: (g, (z - 1) % NZ, y, c))
Z_FAR = pairs_of(lambda g, z, y, c: (g, (z + 2) % NZ, y, c))


def send(array, pairs):
    return lax.ppermute(array, AXES, pairs)


def whole():
    return pl.BlockSpec(memory_space=pltpu.VMEM)


def scalars():
    return pl.BlockSpec(memory_space=pltpu.SMEM)


def in_hbm():
    return pl.BlockSpec(memory_space=pltpu.HBM)


def params():
    return pltpu.CompilerParams(vmem_limit_bytes=VMEM_LIMIT)


LITTLE = pl.CostEstimate(flops=1, bytes_accessed=1, transcendentals=0)


def dequantize_shard(place, quant_codes, block_scales):
    rows, columns = quant_codes.shape
    half = rows // 2

    def kernel(place_ref, codes_ref, scales_ref, own_ref, first_ref):
        g = place_ref[0]
        for i in range(rows // BLOCK):
            source = lax.rem(g * (half // BLOCK) + i, rows // BLOCK)
            start = pl.multiple_of(source * BLOCK, BLOCK)
            for j in range(columns // BLOCK):
                at = slice(j * BLOCK, (j + 1) * BLOCK)
                block = codes_ref[pl.ds(start, BLOCK), at].astype(jnp.float32)
                block = (block * scales_ref[source, j]).astype(jnp.bfloat16)
                own_ref[i * BLOCK : (i + 1) * BLOCK, at] = block
                if i < half // BLOCK:
                    first_ref[i * BLOCK : (i + 1) * BLOCK, at] = block

    return pl.pallas_call(
        kernel,
        out_shape=[
            jax.ShapeDtypeStruct((rows, columns), jnp.bfloat16),
            jax.ShapeDtypeStruct((half, columns), jnp.bfloat16),
        ],
        in_specs=[scalars(), whole(), scalars()],
        out_specs=[whole()] * 2,
        compiler_params=params(),
        cost_estimate=LITTLE,
        name="dequantize",
    )(place, quant_codes, block_scales)


def local_gradients(place, activations, down_t, up, cotangent):
    tokens, width = activations.shape
    rank, features = up.shape
    chips = NZ * 2
    chunk = width // chips
    part = chunk // 2
    up_part = features // 2
    packed = chips * part + up_part

    def kernel(
        place_ref, act_hbm, down_ref, up_ref, cot_ref, latent_ref, lgrad_ref, terms_ref,
        act_ref, total, lgrad_t, sems,
    ):
        y, c = place_ref[2], place_ref[3]
        copies = []
        for i in range(chips):
            at = slice(i * chunk, (i + 1) * chunk)
            copies.append(pltpu.make_async_copy(act_hbm.at[:, at], act_ref.at[i], sems.at[i]))
            copies[-1].start()
        lgrad_ref[...] = weight_transpose(cot_ref[...], up_ref[...]).astype(jnp.bfloat16)
        lgrad_t[...] = weight_transpose(up_ref[...], cot_ref[...]).astype(jnp.bfloat16)
        for i in range(chips):
            copies[i].wait()
            term = jnp.dot(lgrad_t[...], act_ref[i], preferred_element_type=jnp.float32)
            here = jnp.where(i % 2 == y, NZ, 0) + i // 2
            at = pl.ds(pl.multiple_of(here * part, part), part)
            terms_ref[c, :, at] = term[:, :part]
            terms_ref[1 - c, :, at] = term[:, part:]
            latent = weight_transpose(act_ref[i], down_ref[:, i * chunk : (i + 1) * chunk])
            if i == 0:
                total[...] = latent
            else:
                total[...] += latent
        latent_ref[...] = total[...].astype(jnp.bfloat16)
        term = leading(latent_ref[...], cot_ref[...])
        terms_ref[c, :, chips * part :] = term[:, :up_part]
        terms_ref[1 - c, :, chips * part :] = term[:, up_part:]

    return pl.pallas_call(
        kernel,
        out_shape=[
            jax.ShapeDtypeStruct((tokens, rank), jnp.bfloat16),
            jax.ShapeDtypeStruct((tokens, rank), jnp.bfloat16),
            jax.ShapeDtypeStruct((2, rank, packed), jnp.float32),
        ],
        in_specs=[scalars(), in_hbm()] + [whole()] * 3,
        out_specs=[whole()] * 3,
        scratch_shapes=[
            pltpu.VMEM((chips, tokens, chunk), jnp.bfloat16),
            pltpu.VMEM((tokens, rank), jnp.float32),
            pltpu.VMEM((rank, tokens), jnp.bfloat16),
            pltpu.SemaphoreType.DMA((chips,)),
        ],
        compiler_params=params(),
        cost_estimate=LITTLE,
        name="local_gradients",
    )(place, activations, down_t, up, cotangent)


def fold(array):
    rank = array.shape[0]
    return jnp.concatenate([array[: rank // 2], array[rank // 2 :]], axis=1)


def add_cores(own, came, up_part):
    rank, packed = own.shape
    part = (packed - up_part) // (2 * NZ)

    def kernel(own_ref, came_ref, message_ref, kept_ref):
        for z in range(NZ):
            to = slice(z * rank, (z + 1) * rank)
            at = slice(z * part, (z + 1) * part)
            message_ref[to, :] = (own_ref[:, at] + came_ref[:, at]).astype(jnp.bfloat16)
            at = slice((NZ + z) * part, (NZ + z + 1) * part)
            kept_ref[to, :] = own_ref[:, at] + came_ref[:, at]
        at = slice(2 * NZ * part, None)
        message_ref[NZ * rank :, :] = fold(own_ref[:, at] + came_ref[:, at]).astype(jnp.bfloat16)

    return pl.pallas_call(
        kernel,
        out_shape=[
            jax.ShapeDtypeStruct((NZ * rank + rank // 2, part), jnp.bfloat16),
            jax.ShapeDtypeStruct((NZ * rank, part), jnp.float32),
        ],
        in_specs=[whole()] * 2,
        out_specs=[whole()] * 2,
        compiler_params=params(),
        cost_estimate=LITTLE,
        name="add_cores",
    )(own, came)


def multiply(
    place, pieces, activations, down_t, cotangent, lgrad, begin=None, so_far=None, end=None
):
    tokens, width = activations.shape
    features = cotangent.shape[1]
    arrays = []
    for array, _, _ in pieces:
        if not any(array is other for other in arrays):
            arrays.append(array)
    where = [next(i for i, a in enumerate(arrays) if a is array) for array, _, _ in pieces]
    count = len(pieces)
    rows = width // (NZ * 2 * 2 * 2)

    def kernel(*refs):
        refs = list(refs)
        place_ref, act_ref, down_ref, cot_ref, lgrad_ref, one_ref, two_ref = refs[:7]
        del refs[:7]
        if end is not None:
            up_refs = refs[:2]
            del refs[:2]
        array_refs = refs[: len(arrays)]
        del refs[: len(arrays)]
        out_ref, grad_ref = refs[:2]
        sums, grads, out_sems = refs[-3:]
        g, z, y, c = (place_ref[i] for i in range(4))
        columns, weights, going = [], [], []
        for p, (_, first, (dz, dy, dc, dh)) in enumerate(pieces):
            chip = lax.rem(z + (NZ - dz), NZ) * 2 + (1 - y if dy else y)
            device = chip * 2 + (1 - c if dc else c)
            start = (device * 2 + (1 - g if dh else g)) * rows
            columns.append(pl.ds(pl.multiple_of(start, rows), rows))
            weights.append(array_refs[where[p]].at[first : first + rows, :])
        for p in range(count):
            grads[p] = (
                weight_transpose(cot_ref[...], weights[p][...])
                + lowrank_scale
                * jnp.dot(
                    lgrad_ref[...], down_ref[:, columns[p]], preferred_element_type=jnp.float32
                )
            ).astype(jnp.bfloat16)
            copy = pltpu.make_async_copy(grads.at[p], grad_ref.at[:, columns[p]], out_sems.at[p])
            copy.start()
            going.append(copy)
        if begin is not None:
            sums[...] = lowrank_scale * jnp.dot(
                one_ref[...], two_ref[...], preferred_element_type=jnp.float32
            )
        else:
            sums[...] = one_ref[...]
        for p in range(count):
            sums[...] += jnp.dot(
                act_ref[:, columns[p]], weights[p][...], preferred_element_type=jnp.float32
            )
        out_ref[...] = sums[...].astype(out_ref.dtype)
        if end is not None:
            up_part = features // 2
            rank = down_ref.shape[0]
            for ref, core in zip(up_refs, (c, 1 - c), strict=True):
                at = pl.ds(pl.multiple_of(core * up_part, up_part), up_part)
                refs[2][: rank // 2, at] = ref[:, :up_part]
                refs[2][rank // 2 :, at] = ref[:, up_part:]
        for copy in going:
            copy.wait()

    operands = [place, activations, down_t, cotangent, lgrad]
    specs = [scalars()] + [whole()] * 4
    out_shape = [
        jax.ShapeDtypeStruct((tokens, features), jnp.float32 if end is None else jnp.bfloat16),
        jax.ShapeDtypeStruct((tokens, width), jnp.bfloat16),
    ]
    out_specs = [whole(), in_hbm()]
    aliases = {}
    if begin is not None:
        operands += begin
        specs += [whole()] * 2
    else:
        operands += so_far
        specs += [whole(), in_hbm()]
        aliases = {6: 1}
    if end is not None:
        operands += end
        specs += [whole()] * 2
        out_shape.append(jax.ShapeDtypeStruct((down_t.shape[0], features), jnp.float32))
        out_specs.append(whole())
    return pl.pallas_call(
        kernel,
        out_shape=out_shape,
        in_specs=specs + [whole()] * len(arrays),
        out_specs=out_specs,
        scratch_shapes=[
            pltpu.VMEM((tokens, features), jnp.float32),
            pltpu.VMEM((count, tokens, rows), jnp.bfloat16),
            pltpu.SemaphoreType.DMA((count,)),
        ],
        input_output_aliases=aliases,
        compiler_params=params(),
        cost_estimate=LITTLE,
        name="multiply",
    )(*operands, *arrays)


def per_device(
    activations, quant_codes, block_scales, lowrank_down_factor, lowrank_up_factor, cotangent
):
    g = lax.axis_index("groups")
    f = lax.axis_index("fsdp")
    place = jnp.stack([g, f >> 2, (f >> 1) & 1, f & 1]).astype(jnp.int32)
    half = quant_codes.shape[0] // 2
    up_part = lowrank_up_factor.shape[1] // 2
    down_t = lowrank_down_factor.T
    factor = lowrank_scale / math.sqrt(activations.shape[0] * lax.axis_size("fsdp"))
    barrier = lax.optimization_barrier
    join = lambda *arrays: jnp.concatenate(arrays, axis=0)

    def products(pieces, **more):
        return multiply(place, pieces, activations, down_t, cotangent, lgrad, **more)

    def listed(array, dc, *keys):
        return [(array, i * half, (dz, dy, dc, dh)) for i, (dz, dy, dh) in enumerate(keys)]

    def block(body, *operands):
        def never(*operands):
            shapes = jax.eval_shape(body, *operands)
            return jax.tree.map(lambda shape: jnp.zeros(shape.shape, shape.dtype), shapes)

        return lax.cond(place[0] >= 0, body, never, *operands)

    own, first = dequantize_shard(place, quant_codes, block_scales)
    own, first, place = barrier((own, first, place))

    def swap(*arrays):
        return block(lambda *parts: send(join(*parts), OVER_CORE), *arrays)

    down1, up1, y1 = send(first, Z_DOWN), send(first, Z_UP), send(own[half:], OVER_Y)

    def lowrank(place):
        latent, lgrad, terms = local_gradients(
            place, activations, down_t, lowrank_up_factor, cotangent
        )
        terms_y, kept = add_cores(terms[0], send(terms[1], OVER_CORE), up_part)
        return latent, lgrad, terms_y, kept

    latent, lgrad, terms_y, kept = block(lowrank, place)
    came_y = send(terms_y, OVER_Y)
    down1, up1, y1, kept = barrier((down1, up1, y1, kept))

    y2, x2 = send(join(up1, first), OVER_Y), send(join(up1, down1), OVER_X)
    down2 = send(y1, Z_DOWN)
    rank = down_t.shape[0]
    z = place[1]
    summed = kept + came_y[: NZ * rank].astype(jnp.float32)
    summed_up = terms_y[NZ * rank :].astype(jnp.float32) + came_y[NZ * rank :].astype(jnp.float32)
    summed_up = summed_up.astype(jnp.bfloat16)

    def part_of(shift):
        return lax.dynamic_slice_in_dim(summed, ((z + shift) & (NZ - 1)) * rank, rank)

    own_part, next_part = part_of(0), part_of(1)
    far_part = join(part_of(2).astype(jnp.bfloat16), summed_up)
    last_part = join(part_of(3).astype(jnp.bfloat16), summed_up)
    up2 = send(join(up1, far_part), Z_UP)
    swap2 = swap(own, up1, down1, y1)
    keys = [(0, 0, 0), (0, 0, 1), (1, 0, 0), (3, 0, 0), (0, 1, 1)]
    done = products(
        listed(own, 0, *keys[:2])
        + listed(up1, 0, keys[2])
        + listed(down1, 0, keys[3])
        + listed(y1, 0, keys[4])
        + listed(swap2, 1, *keys),
        begin=[latent, lowrank_up_factor],
    )
    y2, x2, down2, up2, own_part, next_part, last_part, summed_up, done = barrier(
        (y2, x2, down2, up2, own_part, next_part, last_part, summed_up, done)
    )

    y3, x3 = send(join(down1, up2[:half]), OVER_Y), send(join(up2[:half], y2[:half]), OVER_X)
    down3 = send(join(down2, last_part), Z_DOWN)
    came_up = up2[half:]
    next_part = next_part + came_up[:rank].astype(jnp.float32)
    up3 = send(join(next_part.astype(jnp.bfloat16), came_up[rank:]), Z_UP)
    swap3 = swap(y2, x2, up2[:half], down2)
    keys = [(1, 1, 0), (0, 1, 0), (1, 0, 1), (3, 0, 1), (2, 0, 0), (3, 1, 1)]
    done = products(
        listed(y2, 0, *keys[:2])
        + listed(x2, 0, *keys[2:4])
        + listed(up2, 0, keys[4])
        + listed(down2, 0, keys[5])
        + listed(swap3, 1, *keys),
        so_far=done,
    )
    y3, x3, down3, up3, came_up, own_part, summed_up, done = barrier(
        (y3, x3, down3, up3, came_up, own_part, summed_up, done)
    )

    swap4 = send(join(y3, x3, down3[:half]), OVER_CORE)
    wide = lambda array: array.astype(jnp.float32)
    up_own = factor * (
        (wide(summed_up) + wide(up3[rank:])) + (wide(came_up[rank:]) + wide(down3[half + rank :]))
    )
    up_came = send(up_own, OVER_CORE)
    grad_down_t = factor * (own_part + (wide(up3[:rank]) + wide(down3[half : half + rank])))
    keys = [(3, 1, 0), (2, 1, 0), (2, 0, 1), (1, 1, 1), (2, 1, 1)]
    done = products(
        listed(y3, 0, *keys[:2]) + listed(x3, 0, *keys[2:4]) + listed(down3, 0, keys[4]),
        so_far=done,
    )
    projected, gradient, grad_up = products(
        listed(swap4, 1, *keys), so_far=done, end=[up_own, up_came]
    )
    return (projected, gradient, grad_down_t.T, grad_up)


def solution(mesh):
    in_specs = (
        P(("groups", "fsdp"), None),
        P("fsdp", None),
        P("fsdp", None),
        P("groups", None),
        P("groups", None),
        P(("groups", "fsdp"), None),
    )
    out_specs = (
        P(("groups", "fsdp"), None),
        P(("groups", "fsdp"), None),
        P(("groups", "fsdp"), None),
        P("groups", None),
    )
    small = mesh.shape["groups"] == 2 and mesh.shape["fsdp"] == NZ * 4
    return jax.shard_map(
        per_device if small else per_device_general,
        mesh=mesh,
        in_specs=in_specs,
        out_specs=out_specs,
        check_vma=False,
    )
```

```python
import math

import jax
import jax.numpy as jnp
from jax import lax
from jax.experimental import pallas as pl
from jax.experimental.pallas import tpu as pltpu
from jax.sharding import PartitionSpec as P

BLOCK = 128
AXES = ("groups", "fsdp")

lowrank_scale = 0.5


def weight_transpose(left, right):
    return lax.dot_general(
        left, right, (((1,), (1,)), ((), ())), preferred_element_type=jnp.float32
    )


def leading(left, right):
    return lax.dot_general(
        left, right, (((0,), (0,)), ((), ())), preferred_element_type=jnp.float32
    )


def dequantize(quant_codes, block_scales):
    spread_scales = jnp.repeat(jnp.repeat(block_scales, BLOCK, axis=0), BLOCK, axis=1)
    return (quant_codes.astype(jnp.float32) * spread_scales).astype(jnp.bfloat16)


def per_device_general(
    activations, quant_codes, block_scales, lowrank_down_factor, lowrank_up_factor, cotangent
):
    value_weight = dequantize(quant_codes, block_scales)
    lowrank_hidden = jnp.dot(
        activations, lowrank_down_factor, preferred_element_type=jnp.float32
    ).astype(jnp.bfloat16)
    lowrank_update = lowrank_scale * jnp.dot(
        lowrank_hidden, lowrank_up_factor, preferred_element_type=jnp.float32
    )
    hidden_gradient = weight_transpose(cotangent, lowrank_up_factor).astype(jnp.bfloat16)
    gathered = lax.all_gather(value_weight, "fsdp", axis=0, tiled=True)
    projected = (
        lowrank_update + jnp.dot(activations, gathered, preferred_element_type=jnp.float32)
    ).astype(jnp.bfloat16)
    input_gradient = (
        weight_transpose(cotangent, gathered)
        + lowrank_scale * weight_transpose(hidden_gradient, lowrank_down_factor)
    ).astype(jnp.bfloat16)
    scaling_factor = lowrank_scale / math.sqrt(activations.shape[0] * lax.axis_size("fsdp"))
    grad_down = lax.psum_scatter(
        scaling_factor * leading(activations, hidden_gradient),
        "fsdp",
        scatter_dimension=0,
        tiled=True,
    )
    grad_up = lax.psum(scaling_factor * leading(lowrank_hidden, cotangent), "fsdp")
    return (projected, input_gradient, grad_down, grad_up)


NZ = 4
VMEM_LIMIT = 24 * 1024 * 1024


def pairs_of(move):
    found = []
    for g in range(2):
        for z in range(NZ):
            for y in range(2):
                for c in range(2):
                    to = move(g, z, y, c)
                    found.append((index_of(g, z, y, c), index_of(*to)))
    return found


def index_of(g, z, y, c):
    return ((g * NZ + z) * 2 + y) * 2 + c


OVER_CORE = pairs_of(lambda g, z, y, c: (g, z, y, 1 - c))
OVER_Y = pairs_of(lambda g, z, y, c: (g, z, 1 - y, c))
OVER_X = pairs_of(lambda g, z, y, c: (1 - g, z, y, c))
Z_UP = pairs_of(lambda g, z, y, c: (g, (z + 1) % NZ, y, c))
Z_DOWN = pairs_of(lambda g, z, y, c: (g, (z - 1) % NZ, y, c))
Z_FAR = pairs_of(lambda g, z, y, c: (g, (z + 2) % NZ, y, c))


def send(array, pairs):
    return lax.ppermute(array, AXES, pairs)


def whole():
    return pl.BlockSpec(memory_space=pltpu.VMEM)


def scalars():
    return pl.BlockSpec(memory_space=pltpu.SMEM)


def in_hbm():
    return pl.BlockSpec(memory_space=pltpu.HBM)


def params():
    return pltpu.CompilerParams(vmem_limit_bytes=VMEM_LIMIT)


LITTLE = pl.CostEstimate(flops=1, bytes_accessed=1, transcendentals=0)


def dequantize_shard(place, quant_codes, block_scales):
    rows, columns = quant_codes.shape
    half = rows // 2

    def kernel(place_ref, codes_ref, scales_ref, own_ref, first_ref):
        g = place_ref[0]
        for i in range(rows // BLOCK):
            source = lax.rem(g * (half // BLOCK) + i, rows // BLOCK)
            start = pl.multiple_of(source * BLOCK, BLOCK)
            for j in range(columns // BLOCK):
                at = slice(j * BLOCK, (j + 1) * BLOCK)
                block = codes_ref[pl.ds(start, BLOCK), at].astype(jnp.float32)
                block = (block * scales_ref[source, j]).astype(jnp.bfloat16)
                own_ref[i * BLOCK : (i + 1) * BLOCK, at] = block
                if i < half // BLOCK:
                    first_ref[i * BLOCK : (i + 1) * BLOCK, at] = block

    return pl.pallas_call(
        kernel,
        out_shape=[
            jax.ShapeDtypeStruct((rows, columns), jnp.bfloat16),
            jax.ShapeDtypeStruct((half, columns), jnp.bfloat16),
        ],
        in_specs=[scalars(), whole(), scalars()],
        out_specs=[whole()] * 2,
        compiler_params=params(),
        cost_estimate=LITTLE,
        name="dequantize",
    )(place, quant_codes, block_scales)


def local_gradients(place, activations, down_t, up, cotangent, other_act, other_cot):
    tokens, width = activations.shape
    rank, features = up.shape
    chips = NZ * 2
    chunk = width // chips
    part = chunk // 2

    def kernel(
        place_ref, act_hbm, down_hbm, up_hbm, cot_hbm, other_hbm, other_cot_hbm, latent_ref,
        lgrad_ref, message_ref, kept_ref, act_ref, down_ref, up_ref, cot_ref, other_ref,
        other_cot_ref, total, lgrad_t, other_t, sums, sems,
    ):
        y, c = place_ref[2], place_ref[3]
        copies = []

        def fetch(source, target):
            copies.append(pltpu.make_async_copy(source, target, sems.at[len(copies)]))
            copies[-1].start()

        for source, target in (
            (up_hbm, up_ref), (cot_hbm, cot_ref), (other_cot_hbm, other_cot_ref),
        ):
            fetch(source, target)
        for i in range(chips):
            at = slice(i * chunk, (i + 1) * chunk)
            mine = pl.ds(pl.multiple_of((2 * i + c) * part, part), part)
            fetch(act_hbm.at[:, at], act_ref.at[i])
            fetch(other_hbm.at[:, mine], other_ref.at[i])
            fetch(down_hbm.at[:, at], down_ref.at[i])
        for copy in copies[:3]:
            copy.wait()
        lgrad_ref[...] = weight_transpose(cot_ref[...], up_ref[...]).astype(jnp.bfloat16)
        lgrad_t[...] = weight_transpose(up_ref[...], cot_ref[...]).astype(jnp.bfloat16)
        other_t[...] = weight_transpose(up_ref[...], other_cot_ref[...]).astype(jnp.bfloat16)
        mine = pl.ds(pl.multiple_of(c * part, part), part)
        for i in range(chips):
            for copy in copies[3 * i + 3 : 3 * i + 6]:
                copy.wait()
            sums[i % 2, i // 2 * rank : (i // 2 + 1) * rank, :] = jnp.dot(
                lgrad_t[...], act_ref[i, :, mine], preferred_element_type=jnp.float32
            ) + jnp.dot(other_t[...], other_ref[i], preferred_element_type=jnp.float32)
            latent = weight_transpose(act_ref[i], down_ref[i])
            if i == 0:
                total[...] = latent
            else:
                total[...] += latent
        message_ref[: NZ * rank, :] = sums[1 - y].astype(jnp.bfloat16)
        kept_ref[...] = sums[y]
        latent_ref[...] = total[...].astype(jnp.bfloat16)
        message_ref[NZ * rank :, :] = leading(latent_ref[...], cot_ref[...]).astype(jnp.bfloat16)

    bf16 = jnp.bfloat16
    return pl.pallas_call(
        kernel,
        out_shape=[
            jax.ShapeDtypeStruct((tokens, rank), bf16),
            jax.ShapeDtypeStruct((tokens, rank), bf16),
            jax.ShapeDtypeStruct(((NZ + 1) * rank, part), bf16),
            jax.ShapeDtypeStruct((NZ * rank, part), jnp.float32),
        ],
        in_specs=[scalars()] + [in_hbm()] * 6,
        out_specs=[whole()] * 4,
        scratch_shapes=[
            pltpu.VMEM((chips, tokens, chunk), bf16),
            pltpu.VMEM((chips, rank, chunk), bf16),
            pltpu.VMEM((rank, features), bf16),
            pltpu.VMEM((tokens, features), bf16),
            pltpu.VMEM((chips, tokens, part), bf16),
            pltpu.VMEM((tokens, features), bf16),
            pltpu.VMEM((tokens, rank), jnp.float32),
            pltpu.VMEM((rank, tokens), bf16),
            pltpu.VMEM((rank, tokens), bf16),
            pltpu.VMEM((2, NZ * rank, part), jnp.float32),
            pltpu.SemaphoreType.DMA((3 * chips + 3,)),
        ],
        compiler_params=pltpu.CompilerParams(vmem_limit_bytes=50 * 1024 * 1024),
        cost_estimate=LITTLE,
        name="local_gradients",
    )(place, activations, down_t, up, cotangent, other_act, other_cot)


def add_y(place, kept, sent, came):
    rows, part = kept.shape
    rank = rows // NZ

    def kernel(place_ref, kept_ref, sent_ref, came_ref, own_ref, next_ref, far_ref, last_ref):
        z = place_ref[1]
        f32 = jnp.float32
        tail = sent_ref[rows:, :].astype(f32) + came_ref[rows:, :].astype(f32)
        for shift, out_ref in enumerate((own_ref, next_ref, far_ref, last_ref)):
            at = pl.ds(pl.multiple_of(lax.rem(z + shift, NZ) * rank, rank), rank)
            summed = kept_ref[at, :] + came_ref[at, :].astype(f32)
            out_ref[:rank, :] = summed.astype(out_ref.dtype)
            if shift >= 2:
                out_ref[rank:, :] = tail.astype(jnp.bfloat16)

    return pl.pallas_call(
        kernel,
        out_shape=[jax.ShapeDtypeStruct((rank, part), jnp.float32)] * 2
        + [jax.ShapeDtypeStruct((2 * rank, part), jnp.bfloat16)] * 2,
        in_specs=[scalars()] + [whole()] * 3,
        out_specs=[whole()] * 4,
        compiler_params=params(),
        cost_estimate=pl.CostEstimate(flops=20000000000, bytes_accessed=1, transcendentals=0),
        name="add_y",
    )(place, kept, sent, came)


def multiply(
    place, pieces, activations, down_t, cotangent, lgrad, factor, begin=None, so_far=None, end=None
):
    tokens, width = activations.shape
    features = cotangent.shape[1]
    arrays = []
    for array, _, _ in pieces:
        if not any(array is other for other in arrays):
            arrays.append(array)
    where = [next(i for i, a in enumerate(arrays) if a is array) for array, _, _ in pieces]
    count = len(pieces)
    rows = width // (NZ * 2 * 2 * 2)

    def kernel(*refs):
        refs = list(refs)
        place_ref, act_ref, down_ref, cot_ref, lgrad_ref, one_ref, two_ref = refs[:7]
        del refs[:7]
        if end is not None:
            terms = refs[:5]
            del refs[:5]
        array_refs = refs[: len(arrays)]
        del refs[: len(arrays)]
        out_ref, grad_ref = refs[:2]
        sums, grads, out_sems = refs[-3:]
        g, z, y, c = (place_ref[i] for i in range(4))
        columns, weights, going = [], [], []
        for p, (_, first, (dz, dy, dc, dh)) in enumerate(pieces):
            chip = lax.rem(z + (NZ - dz), NZ) * 2 + (1 - y if dy else y)
            device = chip * 2 + (1 - c if dc else c)
            start = (device * 2 + (1 - g if dh else g)) * rows
            columns.append(pl.ds(pl.multiple_of(start, rows), rows))
            weights.append(array_refs[where[p]].at[first : first + rows, :])

        def give(source, target):
            going.append(pltpu.make_async_copy(source, target, out_sems.at[len(going)]))
            going[-1].start()

        def backward():
            for p in range(count):
                grads[p] = (
                    weight_transpose(cot_ref[...], weights[p][...])
                    + lowrank_scale
                    * jnp.dot(
                        lgrad_ref[...], down_ref[:, columns[p]], preferred_element_type=jnp.float32
                    )
                ).astype(jnp.bfloat16)
                give(grads.at[p], grad_ref.at[:, columns[p]])

        def forward():
            if begin is not None:
                sums[...] = lowrank_scale * jnp.dot(
                    one_ref[...], two_ref[...], preferred_element_type=jnp.float32
                )
            else:
                sums[...] = one_ref[...]
            for p in range(count):
                sums[...] += jnp.dot(
                    act_ref[:, columns[p]], weights[p][...], preferred_element_type=jnp.float32
                )

        if end is None:
            backward()
            forward()
            out_ref[...] = sums[...]
        else:
            up_out, down_out, rounded, up_sum, down_sum = refs[2:7]
            up_sum[...] = terms[0][...] + terms[1][...]
            give(up_sum, up_out)
            rank = down_ref.shape[0]
            down_sum[...] = factor * (
                terms[2][...]
                + terms[3][:rank, :].astype(jnp.float32)
                + terms[4][rows : rows + rank, :].astype(jnp.float32)
            )
            give(down_sum, down_out)
            forward()
            rounded[...] = sums[...].astype(jnp.bfloat16)
            give(rounded, out_ref)
            backward()
        for copy in going:
            copy.wait()

    operands = [place, activations, down_t, cotangent, lgrad]
    specs = [scalars()] + [whole()] * 4
    out_shape = [
        jax.ShapeDtypeStruct((tokens, features), jnp.float32 if end is None else jnp.bfloat16),
        jax.ShapeDtypeStruct((tokens, width), jnp.bfloat16),
    ]
    out_specs = [whole() if end is None else in_hbm(), in_hbm()]
    scratch = [] if end is None else [pltpu.VMEM((tokens, features), jnp.bfloat16)]
    aliases = {}
    if begin is not None:
        operands += begin
        specs += [whole()] * 2
    else:
        operands += so_far
        specs += [whole(), in_hbm()]
        aliases = {6: 1}
    if end is not None:
        operands += end
        specs += [whole()] * 5
        for term in (end[0], end[2]):
            out_shape.append(jax.ShapeDtypeStruct(term.shape, jnp.float32))
            out_specs.append(in_hbm())
            scratch.append(pltpu.VMEM(term.shape, jnp.float32))
    return pl.pallas_call(
        kernel,
        out_shape=out_shape,
        in_specs=specs + [whole()] * len(arrays),
        out_specs=out_specs,
        scratch_shapes=scratch
        + [
            pltpu.VMEM((tokens, features), jnp.float32),
            pltpu.VMEM((count, tokens, rows), jnp.bfloat16),
            pltpu.SemaphoreType.DMA((count + 3,)),
        ],
        input_output_aliases=aliases,
        compiler_params=params(),
        cost_estimate=LITTLE,
        name="multiply",
    )(*operands, *arrays)


def per_device(
    activations, quant_codes, block_scales, lowrank_down_factor, lowrank_up_factor, cotangent
):
    g = lax.axis_index("groups")
    f = lax.axis_index("fsdp")
    place = jnp.stack([g, f >> 2, (f >> 1) & 1, f & 1]).astype(jnp.int32)
    half = quant_codes.shape[0] // 2
    down_t = lowrank_down_factor.T
    factor = lowrank_scale / math.sqrt(activations.shape[0] * lax.axis_size("fsdp"))
    barrier = lax.optimization_barrier
    join = lambda *arrays: jnp.concatenate(arrays, axis=0)

    def products(pieces, **more):
        return multiply(place, pieces, activations, down_t, cotangent, lgrad, factor, **more)

    def listed(array, dc, *keys):
        return [(array, i * half, (dz, dy, dc, dh)) for i, (dz, dy, dh) in enumerate(keys)]

    own, first = dequantize_shard(place, quant_codes, block_scales)
    own, first, place = barrier((own, first, place))

    def swap(*arrays):
        return send(join(*arrays), OVER_CORE)

    down1, up1, y1 = send(first, Z_DOWN), send(first, Z_UP), send(own[half:], OVER_Y)

    other_act, other_cot = send(activations, OVER_CORE), send(cotangent, OVER_CORE)
    latent, lgrad, terms_y, kept = local_gradients(
        place, activations, down_t, lowrank_up_factor, cotangent, other_act, other_cot
    )
    came_y = send(terms_y, OVER_Y)
    down1, up1, y1, kept = barrier((down1, up1, y1, kept))

    down2 = send(join(y1, down1), Z_DOWN)
    y2, x2 = send(join(up1, first), OVER_Y), send(join(up1, down1), OVER_X)
    rank = down_t.shape[0]
    own_part, next_part, far_part, last_part = add_y(place, kept, terms_y, came_y)
    came_up = send(far_part, Z_UP)
    swap2 = swap(up1, down1, y1)
    own_keys = [(0, 0, 0), (0, 0, 1)]
    keys = [(1, 0, 0), (3, 0, 0), (0, 1, 1)]
    done = products(
        listed(own, 0, *own_keys)
        + listed(up1, 0, keys[0])
        + listed(down1, 0, keys[1])
        + listed(y1, 0, keys[2])
        + listed(swap2, 1, *keys),
        begin=[latent, lowrank_up_factor],
    )
    y2, x2, down2, came_up, own_part, next_part, last_part, done = barrier(
        (y2, x2, down2, came_up, own_part, next_part, last_part, done)
    )

    two = down2[half:]
    down3 = send(join(down2[:half], last_part), Z_DOWN)
    y3, x3 = send(join(down1, two), OVER_Y), send(join(two, y2[:half]), OVER_X)
    next_part = next_part + came_up[:rank].astype(jnp.float32)
    up3 = send(join(next_part.astype(jnp.bfloat16), came_up[rank:]), Z_UP)
    swap3 = swap(y2, x2, down2, own)
    keys = [(1, 1, 0), (0, 1, 0), (1, 0, 1), (3, 0, 1), (3, 1, 1), (2, 0, 0)]
    done = products(
        listed(y2, 0, *keys[:2])
        + listed(x2, 0, *keys[2:4])
        + listed(down2, 0, *keys[4:])
        + listed(swap3, 1, *keys, *own_keys),
        so_far=done,
    )
    y3, x3, down3, up3, came_up, own_part, last_part, done = barrier(
        (y3, x3, down3, up3, came_up, own_part, last_part, done)
    )

    swap4 = send(join(y3, x3, down3[:half]), OVER_CORE)
    wide = lambda array: array.astype(jnp.float32)
    up_own = factor * (
        (wide(last_part[rank:]) + wide(up3[rank:])) + (wide(came_up[rank:]) + wide(down3[half + rank :]))
    )
    up_came = send(up_own, OVER_CORE)
    keys = [(3, 1, 0), (2, 1, 0), (2, 0, 1), (1, 1, 1), (2, 1, 1)]
    done = products(
        listed(y3, 0, *keys[:2]) + listed(x3, 0, *keys[2:4]) + listed(down3, 0, keys[4]),
        so_far=done,
    )
    projected, gradient, grad_up, grad_down_t = products(
        listed(swap4, 1, *keys), so_far=done, end=[up_own, up_came, own_part, up3, down3]
    )
    return (projected, gradient, grad_down_t.T, grad_up)


def solution(mesh):
    in_specs = (
        P(("groups", "fsdp"), None),
        P("fsdp", None),
        P("fsdp", None),
        P("groups", None),
        P("groups", None),
        P(("groups", "fsdp"), None),
    )
    out_specs = (
        P(("groups", "fsdp"), None),
        P(("groups", "fsdp"), None),
        P(("groups", "fsdp"), None),
        P("groups", None),
    )
    small = mesh.shape["groups"] == 2 and mesh.shape["fsdp"] == NZ * 4
    return jax.shard_map(
        per_device if small else per_device_general,
        mesh=mesh,
        in_specs=in_specs,
        out_specs=out_specs,
        check_vma=False,
    )
```

```python
import math

import jax
import jax.numpy as jnp
from jax import lax
from jax.experimental import pallas as pl
from jax.experimental.pallas import tpu as pltpu
from jax.sharding import PartitionSpec as P

BLOCK = 128
AXES = ("groups", "fsdp")

lowrank_scale = 0.5


def weight_transpose(left, right):
    return lax.dot_general(
        left, right, (((1,), (1,)), ((), ())), preferred_element_type=jnp.float32
    )


def leading(left, right):
    return lax.dot_general(
        left, right, (((0,), (0,)), ((), ())), preferred_element_type=jnp.float32
    )


def dequantize(quant_codes, block_scales):
    spread_scales = jnp.repeat(jnp.repeat(block_scales, BLOCK, axis=0), BLOCK, axis=1)
    return (quant_codes.astype(jnp.float32) * spread_scales).astype(jnp.bfloat16)


def per_device_general(
    activations, quant_codes, block_scales, lowrank_down_factor, lowrank_up_factor, cotangent
):
    value_weight = dequantize(quant_codes, block_scales)
    lowrank_hidden = jnp.dot(
        activations, lowrank_down_factor, preferred_element_type=jnp.float32
    ).astype(jnp.bfloat16)
    lowrank_update = lowrank_scale * jnp.dot(
        lowrank_hidden, lowrank_up_factor, preferred_element_type=jnp.float32
    )
    hidden_gradient = weight_transpose(cotangent, lowrank_up_factor).astype(jnp.bfloat16)
    gathered = lax.all_gather(value_weight, "fsdp", axis=0, tiled=True)
    projected = (
        lowrank_update + jnp.dot(activations, gathered, preferred_element_type=jnp.float32)
    ).astype(jnp.bfloat16)
    input_gradient = (
        weight_transpose(cotangent, gathered)
        + lowrank_scale * weight_transpose(hidden_gradient, lowrank_down_factor)
    ).astype(jnp.bfloat16)
    scaling_factor = lowrank_scale / math.sqrt(activations.shape[0] * lax.axis_size("fsdp"))
    grad_down = lax.psum_scatter(
        scaling_factor * leading(activations, hidden_gradient),
        "fsdp",
        scatter_dimension=0,
        tiled=True,
    )
    grad_up = lax.psum(scaling_factor * leading(lowrank_hidden, cotangent), "fsdp")
    return (projected, input_gradient, grad_down, grad_up)


NZ = 4
VMEM_LIMIT = 24 * 1024 * 1024


def pairs_of(move):
    found = []
    for g in range(2):
        for z in range(NZ):
            for y in range(2):
                for c in range(2):
                    to = move(g, z, y, c)
                    found.append((index_of(g, z, y, c), index_of(*to)))
    return found


def index_of(g, z, y, c):
    return ((g * NZ + z) * 2 + y) * 2 + c


OVER_CORE = pairs_of(lambda g, z, y, c: (g, z, y, 1 - c))
OVER_Y = pairs_of(lambda g, z, y, c: (g, z, 1 - y, c))
OVER_X = pairs_of(lambda g, z, y, c: (1 - g, z, y, c))
Z_UP = pairs_of(lambda g, z, y, c: (g, (z + 1) % NZ, y, c))
Z_DOWN = pairs_of(lambda g, z, y, c: (g, (z - 1) % NZ, y, c))
Z_FAR = pairs_of(lambda g, z, y, c: (g, (z + 2) % NZ, y, c))


def send(array, pairs):
    return lax.ppermute(array, AXES, pairs)


def whole():
    return pl.BlockSpec(memory_space=pltpu.VMEM)


def scalars():
    return pl.BlockSpec(memory_space=pltpu.SMEM)


def in_hbm():
    return pl.BlockSpec(memory_space=pltpu.HBM)


def params():
    return pltpu.CompilerParams(vmem_limit_bytes=VMEM_LIMIT)


LITTLE = pl.CostEstimate(flops=1, bytes_accessed=1, transcendentals=0)


def dequantize_shard(place, quant_codes, block_scales):
    rows, columns = quant_codes.shape
    half = rows // 2

    def kernel(place_ref, codes_ref, scales_ref, own_ref, first_ref):
        g = place_ref[0]
        for i in range(rows // BLOCK):
            source = lax.rem(g * (half // BLOCK) + i, rows // BLOCK)
            start = pl.multiple_of(source * BLOCK, BLOCK)
            for j in range(columns // BLOCK):
                at = slice(j * BLOCK, (j + 1) * BLOCK)
                block = codes_ref[pl.ds(start, BLOCK), at].astype(jnp.float32)
                block = (block * scales_ref[source, j]).astype(jnp.bfloat16)
                own_ref[i * BLOCK : (i + 1) * BLOCK, at] = block
                if i < half // BLOCK:
                    first_ref[i * BLOCK : (i + 1) * BLOCK, at] = block

    return pl.pallas_call(
        kernel,
        out_shape=[
            jax.ShapeDtypeStruct((rows, columns), jnp.bfloat16),
            jax.ShapeDtypeStruct((half, columns), jnp.bfloat16),
        ],
        in_specs=[scalars(), whole(), scalars()],
        out_specs=[whole()] * 2,
        compiler_params=params(),
        cost_estimate=LITTLE,
        name="dequantize",
    )(place, quant_codes, block_scales)


def local_gradients(place, activations, down_t, up, cotangent, other_act, other_cot):
    tokens, width = activations.shape
    rank, features = up.shape
    chips = NZ * 2
    chunk = width // chips
    part = chunk // 2

    def kernel(
        place_ref, act_hbm, down_hbm, up_hbm, cot_hbm, other_hbm, other_cot_hbm, latent_ref,
        lgrad_ref, message_ref, kept_ref, act_ref, down_ref, up_ref, cot_ref, other_ref,
        other_cot_ref, total, lgrad_t, other_t, sums, sems,
    ):
        y, c = place_ref[2], place_ref[3]
        copies = []

        def fetch(source, target):
            copies.append(pltpu.make_async_copy(source, target, sems.at[len(copies)]))
            copies[-1].start()

        for source, target in (
            (up_hbm, up_ref), (cot_hbm, cot_ref), (other_cot_hbm, other_cot_ref),
        ):
            fetch(source, target)
        for i in range(chips):
            at = slice(i * chunk, (i + 1) * chunk)
            mine = pl.ds(pl.multiple_of((2 * i + c) * part, part), part)
            fetch(act_hbm.at[:, at], act_ref.at[i])
            fetch(other_hbm.at[:, mine], other_ref.at[i])
            fetch(down_hbm.at[:, at], down_ref.at[i])
        for copy in copies[:3]:
            copy.wait()
        lgrad_ref[...] = weight_transpose(cot_ref[...], up_ref[...]).astype(jnp.bfloat16)
        lgrad_t[...] = weight_transpose(up_ref[...], cot_ref[...]).astype(jnp.bfloat16)
        other_t[...] = weight_transpose(up_ref[...], other_cot_ref[...]).astype(jnp.bfloat16)
        mine = pl.ds(pl.multiple_of(c * part, part), part)
        for i in range(chips):
            for copy in copies[3 * i + 3 : 3 * i + 6]:
                copy.wait()
            sums[i % 2, i // 2 * rank : (i // 2 + 1) * rank, :] = jnp.dot(
                lgrad_t[...], act_ref[i, :, mine], preferred_element_type=jnp.float32
            ) + jnp.dot(other_t[...], other_ref[i], preferred_element_type=jnp.float32)
            latent = weight_transpose(act_ref[i], down_ref[i])
            if i == 0:
                total[...] = latent
            else:
                total[...] += latent
        message_ref[: NZ * rank, :] = sums[1 - y].astype(jnp.bfloat16)
        kept_ref[...] = sums[y]
        latent_ref[...] = total[...].astype(jnp.bfloat16)
        message_ref[NZ * rank :, :] = leading(latent_ref[...], cot_ref[...]).astype(jnp.bfloat16)

    bf16 = jnp.bfloat16
    return pl.pallas_call(
        kernel,
        out_shape=[
            jax.ShapeDtypeStruct((tokens, rank), bf16),
            jax.ShapeDtypeStruct((tokens, rank), bf16),
            jax.ShapeDtypeStruct(((NZ + 1) * rank, part), bf16),
            jax.ShapeDtypeStruct((NZ * rank, part), jnp.float32),
        ],
        in_specs=[scalars()] + [in_hbm()] * 6,
        out_specs=[whole()] * 4,
        scratch_shapes=[
            pltpu.VMEM((chips, tokens, chunk), bf16),
            pltpu.VMEM((chips, rank, chunk), bf16),
            pltpu.VMEM((rank, features), bf16),
            pltpu.VMEM((tokens, features), bf16),
            pltpu.VMEM((chips, tokens, part), bf16),
            pltpu.VMEM((tokens, features), bf16),
            pltpu.VMEM((tokens, rank), jnp.float32),
            pltpu.VMEM((rank, tokens), bf16),
            pltpu.VMEM((rank, tokens), bf16),
            pltpu.VMEM((2, NZ * rank, part), jnp.float32),
            pltpu.SemaphoreType.DMA((3 * chips + 3,)),
        ],
        compiler_params=pltpu.CompilerParams(vmem_limit_bytes=50 * 1024 * 1024),
        cost_estimate=LITTLE,
        name="local_gradients",
    )(place, activations, down_t, up, cotangent, other_act, other_cot)


def add_y(place, kept, sent, came):
    rows, part = kept.shape
    rank = rows // NZ
    fold = rank // 2
    kinds = [jnp.float32, jnp.float32, jnp.bfloat16, jnp.bfloat16]

    def kernel(place_ref, kept_ref, sent_ref, came_ref, *out_refs):
        z, c = place_ref[1], place_ref[3]
        f32 = jnp.float32
        for shift in range(NZ):
            at = pl.ds(pl.multiple_of(lax.rem(z + shift, NZ) * rank, rank), rank)
            summed = kept_ref[at, :] + came_ref[at, :].astype(f32)
            out_refs[shift][...] = summed.astype(kinds[shift])
        term = sent_ref[rows:, :].astype(f32) + came_ref[rows:, :].astype(f32)
        low, high = term[:, : part // 2], term[:, part // 2 :]
        for core, ref in enumerate(out_refs[NZ:]):
            half = jnp.where(c == core, low, high)
            ref[:, : part // 2] = half[:fold]
            ref[:, part // 2 :] = half[fold:]

    return pl.pallas_call(
        kernel,
        out_shape=[jax.ShapeDtypeStruct((rank, part), kind) for kind in kinds]
        + [jax.ShapeDtypeStruct((fold, part), jnp.float32)] * 2,
        in_specs=[scalars()] + [whole()] * 3,
        out_specs=[whole()] * (NZ + 2),
        compiler_params=params(),
        cost_estimate=pl.CostEstimate(flops=10000000000, bytes_accessed=1, transcendentals=0),
        name="add_y",
    )(place, kept, sent, came)


def multiply(
    place, pieces, activations, down_t, cotangent, lgrad, factor, begin=None, so_far=None, end=None
):
    tokens, width = activations.shape
    features = cotangent.shape[1]
    arrays = []
    for array, *_ in pieces:
        if not any(array is other for other in arrays):
            arrays.append(array)
    where = [next(i for i, a in enumerate(arrays) if a is array) for array, *_ in pieces]
    count = len(pieces)
    rows = width // (NZ * 2 * 2 * 2)

    def kernel(*refs):
        refs = list(refs)
        place_ref, act_ref, down_ref, cot_ref, lgrad_ref, one_ref, two_ref = refs[:7]
        del refs[:7]
        if end is not None:
            terms = refs[:5]
            del refs[:5]
        array_refs = refs[: len(arrays)]
        del refs[: len(arrays)]
        out_ref, grad_ref = refs[:2]
        sums, grads, out_sems = refs[-3:]
        g, z, y, c = (place_ref[i] for i in range(4))
        columns, weights, going = [], [], []
        for p, (_, first, size, offset, (dz, dy, dc, dh)) in enumerate(pieces):
            chip = lax.rem(z + (NZ - dz), NZ) * 2 + (1 - y if dy else y)
            device = chip * 2 + (1 - c if dc else c)
            start = (device * 2 + (1 - g if dh else g)) * rows + offset
            columns.append(pl.ds(pl.multiple_of(start, BLOCK), size))
            weights.append(array_refs[where[p]].at[first : first + size, :])

        def give(source, target):
            going.append(pltpu.make_async_copy(source, target, out_sems.at[len(going)]))
            going[-1].start()

        def backward():
            for p in range(count):
                held = grads.at[p, :, : pieces[p][2]]
                held[...] = (
                    weight_transpose(cot_ref[...], weights[p][...])
                    + lowrank_scale
                    * jnp.dot(
                        lgrad_ref[...], down_ref[:, columns[p]], preferred_element_type=jnp.float32
                    )
                ).astype(jnp.bfloat16)
                give(held, grad_ref.at[:, columns[p]])

        def forward():
            if begin is not None:
                sums[...] = lowrank_scale * jnp.dot(
                    one_ref[...], two_ref[...], preferred_element_type=jnp.float32
                )
            else:
                sums[...] = one_ref[...]
            for p in range(count):
                sums[...] += jnp.dot(
                    act_ref[:, columns[p]], weights[p][...], preferred_element_type=jnp.float32
                )

        if end is None:
            backward()
            forward()
            out_ref[...] = sums[...]
        else:
            up_out, down_out, rounded, up_sum, down_sum = refs[2:7]
            rank = down_ref.shape[0]
            part = features // 2
            for ref, core in zip(terms[:2], (c, 1 - c), strict=True):
                at = pl.ds(pl.multiple_of(core * part, part), part)
                up_sum[: rank // 2, at] = ref[:, :part]
                up_sum[rank // 2 :, at] = ref[:, part:]
            give(up_sum, up_out)
            down_sum[...] = factor * (
                terms[2][...]
                + terms[3][:rank, :].astype(jnp.float32)
                + terms[4][rows : rows + rank, :].astype(jnp.float32)
            )
            give(down_sum, down_out)
            forward()
            rounded[...] = sums[...].astype(jnp.bfloat16)
            give(rounded, out_ref)
            backward()
        for copy in going:
            copy.wait()

    operands = [place, activations, down_t, cotangent, lgrad]
    specs = [scalars()] + [whole()] * 4
    out_shape = [
        jax.ShapeDtypeStruct((tokens, features), jnp.float32 if end is None else jnp.bfloat16),
        jax.ShapeDtypeStruct((tokens, width), jnp.bfloat16),
    ]
    out_specs = [whole() if end is None else in_hbm(), in_hbm()]
    scratch = [] if end is None else [pltpu.VMEM((tokens, features), jnp.bfloat16)]
    aliases = {}
    if begin is not None:
        operands += begin
        specs += [whole()] * 2
    else:
        operands += so_far
        specs += [whole(), in_hbm()]
        aliases = {6: 1}
    if end is not None:
        operands += end
        specs += [whole()] * 5
        for _ in range(2):
            out_shape.append(jax.ShapeDtypeStruct((down_t.shape[0], features), jnp.float32))
            out_specs.append(in_hbm())
            scratch.append(pltpu.VMEM((down_t.shape[0], features), jnp.float32))
    return pl.pallas_call(
        kernel,
        out_shape=out_shape,
        in_specs=specs + [whole()] * len(arrays),
        out_specs=out_specs,
        scratch_shapes=scratch
        + [
            pltpu.VMEM((tokens, features), jnp.float32),
            pltpu.VMEM((count, tokens, rows), jnp.bfloat16),
            pltpu.SemaphoreType.DMA((count + 3,)),
        ],
        input_output_aliases=aliases,
        compiler_params=params(),
        cost_estimate=LITTLE,
        name="multiply",
    )(*operands, *arrays)


def per_device(
    activations, quant_codes, block_scales, lowrank_down_factor, lowrank_up_factor, cotangent
):
    g = lax.axis_index("groups")
    f = lax.axis_index("fsdp")
    place = jnp.stack([g, f >> 2, (f >> 1) & 1, f & 1]).astype(jnp.int32)
    half = quant_codes.shape[0] // 2
    down_t = lowrank_down_factor.T
    factor = lowrank_scale / math.sqrt(activations.shape[0] * lax.axis_size("fsdp"))
    barrier = lax.optimization_barrier
    join = lambda *arrays: jnp.concatenate(arrays, axis=0)

    def products(pieces, **more):
        return multiply(place, pieces, activations, down_t, cotangent, lgrad, factor, **more)

    def piece(array, first, dc, key, size=half, offset=0):
        return (array, first, size, offset, (key[0], key[1], dc, key[2]))

    def listed(array, dc, *keys):
        return [piece(array, i * half, dc, key) for i, key in enumerate(keys)]

    own, first = dequantize_shard(place, quant_codes, block_scales)
    own, first, place = barrier((own, first, place))

    def swap(*arrays):
        return send(join(*arrays), OVER_CORE)

    down1, up1, y1 = send(first, Z_DOWN), send(first, Z_UP), send(own, OVER_Y)
    other_act, other_cot = send(activations, OVER_CORE), send(cotangent, OVER_CORE)
    latent, lgrad, terms_y, kept = local_gradients(
        place, activations, down_t, lowrank_up_factor, cotangent, other_act, other_cot
    )
    came_y = send(terms_y, OVER_Y)
    down1, up1, y1, kept = barrier((down1, up1, y1, kept))

    down2 = send(join(y1[half:], down1), Z_DOWN)
    y2, x2 = send(up1, OVER_Y), send(join(up1, down1), OVER_X)
    rank = down_t.shape[0]
    own_part, next_part, far_part, last_part, up_own, up_away = add_y(
        place, kept, terms_y, came_y
    )
    summed_up = (up_own + send(up_away, OVER_CORE)).astype(jnp.bfloat16)
    came_up = send(join(far_part, summed_up), Z_UP)
    last_part = join(last_part, summed_up)
    swap2 = swap(up1, down1, y1)
    own_keys = [(0, 0, 0), (0, 0, 1)]
    keys = [(1, 0, 0), (3, 0, 0), (0, 1, 0), (0, 1, 1)]
    done = products(
        listed(own, 0, *own_keys)
        + listed(up1, 0, keys[0])
        + listed(down1, 0, keys[1])
        + listed(y1, 0, *keys[2:])
        + listed(swap2, 1, *keys),
        begin=[latent, lowrank_up_factor],
    )
    y2, x2, down2, came_up, own_part, next_part, last_part, done = barrier(
        (y2, x2, down2, came_up, own_part, next_part, last_part, done)
    )

    two = down2[half:]
    down3 = send(join(down2[:half], last_part), Z_DOWN)
    y3, x3 = send(join(down1, two), OVER_Y), send(join(two, y2), OVER_X)
    next_part = next_part + came_up[:rank].astype(jnp.float32)
    up3 = send(join(next_part.astype(jnp.bfloat16), came_up[rank:]), Z_UP)
    swap3 = swap(y2, x2, down2, own)
    keys = [(1, 1, 0), (1, 0, 1), (3, 0, 1), (3, 1, 1), (2, 0, 0)]
    done = products(
        listed(y2, 0, keys[0])
        + listed(x2, 0, *keys[1:3])
        + listed(down2, 0, *keys[3:])
        + listed(swap3, 1, *keys, *own_keys),
        so_far=done,
    )
    y3, x3, down3, up3, came_up, own_part, last_part, done = barrier(
        (y3, x3, down3, up3, came_up, own_part, last_part, done)
    )

    swap4 = send(join(y3, x3, down3[:half]), OVER_CORE)
    wide = lambda array: array.astype(jnp.float32)
    up_own = factor * (
        (wide(last_part[rank:]) + wide(up3[rank:]))
        + (wide(came_up[rank:]) + wide(down3[half + rank :]))
    )
    up_came = send(up_own, OVER_CORE)

    keys = [(3, 1, 0), (2, 1, 0), (2, 0, 1), (1, 1, 1), (2, 1, 1)]
    done = products(
        listed(y3, 0, *keys[:2]) + listed(x3, 0, *keys[2:4]) + listed(down3, 0, keys[4]),
        so_far=done,
    )
    projected, gradient, grad_up, grad_down_t = products(
        listed(swap4, 1, *keys),
        so_far=done,
        end=[up_own, up_came, own_part, up3, down3],
    )
    return (projected, gradient, grad_down_t.T, grad_up)


def solution(mesh):
    in_specs = (
        P(("groups", "fsdp"), None),
        P("fsdp", None),
        P("fsdp", None),
        P("groups", None),
        P("groups", None),
        P(("groups", "fsdp"), None),
    )
    out_specs = (
        P(("groups", "fsdp"), None),
        P(("groups", "fsdp"), None),
        P(("groups", "fsdp"), None),
        P("groups", None),
    )
    small = mesh.shape["groups"] == 2 and mesh.shape["fsdp"] == NZ * 4
    return jax.shard_map(
        per_device if small else per_device_general,
        mesh=mesh,
        in_specs=in_specs,
        out_specs=out_specs,
        check_vma=False,
    )
```

```python
import math

import jax
import jax.numpy as jnp
from jax import lax
from jax.experimental import pallas as pl
from jax.experimental.pallas import tpu as pltpu
from jax.sharding import PartitionSpec as P

BLOCK = 128
AXES = ("groups", "fsdp")

lowrank_scale = 0.5


def weight_transpose(left, right):
    return lax.dot_general(
        left, right, (((1,), (1,)), ((), ())), preferred_element_type=jnp.float32
    )


def leading(left, right):
    return lax.dot_general(
        left, right, (((0,), (0,)), ((), ())), preferred_element_type=jnp.float32
    )


def dequantize(quant_codes, block_scales):
    spread_scales = jnp.repeat(jnp.repeat(block_scales, BLOCK, axis=0), BLOCK, axis=1)
    return (quant_codes.astype(jnp.float32) * spread_scales).astype(jnp.bfloat16)


def per_device_general(
    activations, quant_codes, block_scales, lowrank_down_factor, lowrank_up_factor, cotangent
):
    value_weight = dequantize(quant_codes, block_scales)
    lowrank_hidden = jnp.dot(
        activations, lowrank_down_factor, preferred_element_type=jnp.float32
    ).astype(jnp.bfloat16)
    lowrank_update = lowrank_scale * jnp.dot(
        lowrank_hidden, lowrank_up_factor, preferred_element_type=jnp.float32
    )
    hidden_gradient = weight_transpose(cotangent, lowrank_up_factor).astype(jnp.bfloat16)
    gathered = lax.all_gather(value_weight, "fsdp", axis=0, tiled=True)
    projected = (
        lowrank_update + jnp.dot(activations, gathered, preferred_element_type=jnp.float32)
    ).astype(jnp.bfloat16)
    input_gradient = (
        weight_transpose(cotangent, gathered)
        + lowrank_scale * weight_transpose(hidden_gradient, lowrank_down_factor)
    ).astype(jnp.bfloat16)
    scaling_factor = lowrank_scale / math.sqrt(activations.shape[0] * lax.axis_size("fsdp"))
    grad_down = lax.psum_scatter(
        scaling_factor * leading(activations, hidden_gradient),
        "fsdp",
        scatter_dimension=0,
        tiled=True,
    )
    grad_up = lax.psum(scaling_factor * leading(lowrank_hidden, cotangent), "fsdp")
    return (projected, input_gradient, grad_down, grad_up)


NZ = 4
VMEM_LIMIT = 24 * 1024 * 1024


def pairs_of(move):
    found = []
    for g in range(2):
        for z in range(NZ):
            for y in range(2):
                for c in range(2):
                    to = move(g, z, y, c)
                    found.append((index_of(g, z, y, c), index_of(*to)))
    return found


def index_of(g, z, y, c):
    return ((g * NZ + z) * 2 + y) * 2 + c


OVER_CORE = pairs_of(lambda g, z, y, c: (g, z, y, 1 - c))
OVER_Y = pairs_of(lambda g, z, y, c: (g, z, 1 - y, c))
OVER_X = pairs_of(lambda g, z, y, c: (1 - g, z, y, c))
Z_UP = pairs_of(lambda g, z, y, c: (g, (z + 1) % NZ, y, c))
Z_DOWN = pairs_of(lambda g, z, y, c: (g, (z - 1) % NZ, y, c))
Z_FAR = pairs_of(lambda g, z, y, c: (g, (z + 2) % NZ, y, c))


def position():
    f = lax.axis_index("fsdp")
    return lax.axis_index("groups"), f >> 2, (f >> 1) & 1, f & 1


def send(array, pairs):
    return lax.ppermute(array, AXES, pairs)


def whole():
    return pl.BlockSpec(memory_space=pltpu.VMEM)


def scalars():
    return pl.BlockSpec(memory_space=pltpu.SMEM)


def in_hbm():
    return pl.BlockSpec(memory_space=pltpu.HBM)


def params():
    return pltpu.CompilerParams(vmem_limit_bytes=VMEM_LIMIT)


LITTLE = pl.CostEstimate(flops=1, bytes_accessed=1, transcendentals=0)


def dequantize_shard(quant_codes, block_scales):
    rows, columns = quant_codes.shape
    half = rows // 2

    def kernel(codes_ref, scales_ref, own_ref, first_ref):
        g = position()[0]
        for i in range(rows // BLOCK):
            source = lax.rem(g * (half // BLOCK) + i, rows // BLOCK)
            start = pl.multiple_of(source * BLOCK, BLOCK)
            for j in range(columns // BLOCK):
                at = slice(j * BLOCK, (j + 1) * BLOCK)
                block = codes_ref[pl.ds(start, BLOCK), at].astype(jnp.float32)
                block = (block * scales_ref[source, j]).astype(jnp.bfloat16)
                own_ref[i * BLOCK : (i + 1) * BLOCK, at] = block
                if i < half // BLOCK:
                    first_ref[i * BLOCK : (i + 1) * BLOCK, at] = block

    return pl.pallas_call(
        kernel,
        out_shape=[
            jax.ShapeDtypeStruct((rows, columns), jnp.bfloat16),
            jax.ShapeDtypeStruct((half, columns), jnp.bfloat16),
        ],
        in_specs=[whole(), scalars()],
        out_specs=[whole()] * 2,
        compiler_params=params(),
        cost_estimate=LITTLE,
        name="dequantize",
    )(quant_codes, block_scales)


def local_gradients(activations, down_t, up, cotangent, other_act, other_cot):
    tokens, width = activations.shape
    rank, features = up.shape
    chips = NZ * 2
    chunk = width // chips
    part = chunk // 2

    def kernel(
        act_hbm, down_hbm, up_hbm, cot_hbm, other_hbm, other_cot_hbm, latent_ref,
        lgrad_ref, message_ref, kept_ref, act_ref, down_ref, up_ref, cot_ref, other_ref,
        other_cot_ref, total, lgrad_t, other_t, sums, sems,
    ):
        _, _, y, c = position()
        copies = []

        def fetch(source, target):
            copies.append(pltpu.make_async_copy(source, target, sems.at[len(copies)]))
            copies[-1].start()

        for source, target in (
            (up_hbm, up_ref), (cot_hbm, cot_ref), (other_cot_hbm, other_cot_ref),
        ):
            fetch(source, target)
        for i in range(chips):
            at = slice(i * chunk, (i + 1) * chunk)
            mine = pl.ds(pl.multiple_of((2 * i + c) * part, part), part)
            fetch(act_hbm.at[:, at], act_ref.at[i])
            fetch(other_hbm.at[:, mine], other_ref.at[i])
            fetch(down_hbm.at[:, at], down_ref.at[i])
        for copy in copies[:3]:
            copy.wait()
        lgrad_ref[...] = weight_transpose(cot_ref[...], up_ref[...]).astype(jnp.bfloat16)
        lgrad_t[...] = weight_transpose(up_ref[...], cot_ref[...]).astype(jnp.bfloat16)
        other_t[...] = weight_transpose(up_ref[...], other_cot_ref[...]).astype(jnp.bfloat16)
        mine = pl.ds(pl.multiple_of(c * part, part), part)
        for i in range(chips):
            for copy in copies[3 * i + 3 : 3 * i + 6]:
                copy.wait()
            sums[i % 2, i // 2 * rank : (i // 2 + 1) * rank, :] = jnp.dot(
                lgrad_t[...], act_ref[i, :, mine], preferred_element_type=jnp.float32
            ) + jnp.dot(other_t[...], other_ref[i], preferred_element_type=jnp.float32)
            latent = weight_transpose(act_ref[i], down_ref[i])
            if i == 0:
                total[...] = latent
            else:
                total[...] += latent
        message_ref[: NZ * rank, :] = sums[1 - y].astype(jnp.bfloat16)
        kept_ref[...] = sums[y]
        latent_ref[...] = total[...].astype(jnp.bfloat16)
        message_ref[NZ * rank :, :] = leading(latent_ref[...], cot_ref[...]).astype(jnp.bfloat16)

    bf16 = jnp.bfloat16
    return pl.pallas_call(
        kernel,
        out_shape=[
            jax.ShapeDtypeStruct((tokens, rank), bf16),
            jax.ShapeDtypeStruct((tokens, rank), bf16),
            jax.ShapeDtypeStruct(((NZ + 1) * rank, part), bf16),
            jax.ShapeDtypeStruct((NZ * rank, part), jnp.float32),
        ],
        in_specs=[in_hbm()] * 6,
        out_specs=[whole()] * 4,
        scratch_shapes=[
            pltpu.VMEM((chips, tokens, chunk), bf16),
            pltpu.VMEM((chips, rank, chunk), bf16),
            pltpu.VMEM((rank, features), bf16),
            pltpu.VMEM((tokens, features), bf16),
            pltpu.VMEM((chips, tokens, part), bf16),
            pltpu.VMEM((tokens, features), bf16),
            pltpu.VMEM((tokens, rank), jnp.float32),
            pltpu.VMEM((rank, tokens), bf16),
            pltpu.VMEM((rank, tokens), bf16),
            pltpu.VMEM((2, NZ * rank, part), jnp.float32),
            pltpu.SemaphoreType.DMA((3 * chips + 3,)),
        ],
        compiler_params=pltpu.CompilerParams(vmem_limit_bytes=54 * 1024 * 1024),
        cost_estimate=LITTLE,
        name="local_gradients",
    )(activations, down_t, up, cotangent, other_act, other_cot)


def add_y(kept, sent, came):
    rows, part = kept.shape
    rank = rows // NZ
    fold = rank // 2
    kinds = [jnp.float32, jnp.float32, jnp.bfloat16, jnp.bfloat16]

    def kernel(kept_ref, sent_ref, came_ref, *out_refs):
        _, z, _, c = position()
        f32 = jnp.float32
        for shift in range(NZ):
            at = pl.ds(pl.multiple_of(lax.rem(z + shift, NZ) * rank, rank), rank)
            summed = kept_ref[at, :] + came_ref[at, :].astype(f32)
            out_refs[shift][...] = summed.astype(kinds[shift])
        term = sent_ref[rows:, :].astype(f32) + came_ref[rows:, :].astype(f32)
        low, high = term[:, : part // 2], term[:, part // 2 :]
        for core, ref in enumerate(out_refs[NZ:]):
            half = jnp.where(c == core, low, high)
            ref[:, : part // 2] = half[:fold]
            ref[:, part // 2 :] = half[fold:]

    return pl.pallas_call(
        kernel,
        out_shape=[jax.ShapeDtypeStruct((rank, part), kind) for kind in kinds]
        + [jax.ShapeDtypeStruct((fold, part), jnp.float32)] * 2,
        in_specs=[whole()] * 3,
        out_specs=[whole()] * (NZ + 2),
        compiler_params=params(),
        cost_estimate=pl.CostEstimate(flops=10000000000, bytes_accessed=1, transcendentals=0),
        name="add_y",
    )(kept, sent, came)


def multiply(
    pieces, activations, down_t, cotangent, lgrad, factor, begin=None, so_far=None, end=None
):
    tokens, width = activations.shape
    features = cotangent.shape[1]
    arrays = []
    for array, *_ in pieces:
        if not any(array is other for other in arrays):
            arrays.append(array)
    where = [next(i for i, a in enumerate(arrays) if a is array) for array, *_ in pieces]
    count = len(pieces)
    rows = width // (NZ * 2 * 2 * 2)

    def kernel(*refs):
        refs = list(refs)
        act_ref, down_ref, cot_ref, lgrad_ref, one_ref, two_ref = refs[:6]
        del refs[:6]
        if end is not None:
            terms = refs[:5]
            del refs[:5]
        array_refs = refs[: len(arrays)]
        del refs[: len(arrays)]
        out_ref, grad_ref = refs[:2]
        sums, grads, out_sems = refs[-3:]
        g, z, y, c = position()
        columns, weights, going = [], [], []
        for p, (_, first, size, offset, (dz, dy, dc, dh)) in enumerate(pieces):
            chip = lax.rem(z + (NZ - dz), NZ) * 2 + (1 - y if dy else y)
            device = chip * 2 + (1 - c if dc else c)
            start = (device * 2 + (1 - g if dh else g)) * rows + offset
            columns.append(pl.ds(pl.multiple_of(start, BLOCK), size))
            weights.append(array_refs[where[p]].at[first : first + size, :])

        def give(source, target):
            going.append(pltpu.make_async_copy(source, target, out_sems.at[len(going)]))
            going[-1].start()

        def backward():
            for p in range(count):
                held = grads.at[p, :, : pieces[p][2]]
                held[...] = (
                    weight_transpose(cot_ref[...], weights[p][...])
                    + lowrank_scale
                    * jnp.dot(
                        lgrad_ref[...], down_ref[:, columns[p]], preferred_element_type=jnp.float32
                    )
                ).astype(jnp.bfloat16)
                give(held, grad_ref.at[:, columns[p]])

        def forward():
            if begin is not None:
                sums[...] = lowrank_scale * jnp.dot(
                    one_ref[...], two_ref[...], preferred_element_type=jnp.float32
                )
            else:
                sums[...] = one_ref[...]
            for p in range(count):
                sums[...] += jnp.dot(
                    act_ref[:, columns[p]], weights[p][...], preferred_element_type=jnp.float32
                )

        if end is None:
            backward()
            forward()
            out_ref[...] = sums[...]
        else:
            up_out, down_out, rounded, up_sum, down_sum = refs[2:7]
            rank = down_ref.shape[0]
            part = features // 2
            for ref, core in zip(terms[:2], (c, 1 - c), strict=True):
                at = pl.ds(pl.multiple_of(core * part, part), part)
                up_sum[: rank // 2, at] = ref[:, :part]
                up_sum[rank // 2 :, at] = ref[:, part:]
            give(up_sum, up_out)
            down_sum[...] = factor * (
                terms[2][...]
                + terms[3][:rank, :].astype(jnp.float32)
                + terms[4][rows : rows + rank, :].astype(jnp.float32)
            )
            give(down_sum, down_out)
            forward()
            rounded[...] = sums[...].astype(jnp.bfloat16)
            give(rounded, out_ref)
            backward()
        for copy in going:
            copy.wait()

    operands = [activations, down_t, cotangent, lgrad]
    specs = [whole()] * 4
    out_shape = [
        jax.ShapeDtypeStruct((tokens, features), jnp.float32 if end is None else jnp.bfloat16),
        jax.ShapeDtypeStruct((tokens, width), jnp.bfloat16),
    ]
    out_specs = [whole() if end is None else in_hbm(), in_hbm()]
    scratch = [] if end is None else [pltpu.VMEM((tokens, features), jnp.bfloat16)]
    aliases = {}
    if begin is not None:
        operands += begin
        specs += [whole()] * 2
    else:
        operands += so_far
        specs += [whole(), in_hbm()]
        aliases = {5: 1}
    if end is not None:
        operands += end
        specs += [whole()] * 5
        for _ in range(2):
            out_shape.append(jax.ShapeDtypeStruct((down_t.shape[0], features), jnp.float32))
            out_specs.append(in_hbm())
            scratch.append(pltpu.VMEM((down_t.shape[0], features), jnp.float32))
    return pl.pallas_call(
        kernel,
        out_shape=out_shape,
        in_specs=specs + [whole()] * len(arrays),
        out_specs=out_specs,
        scratch_shapes=scratch
        + [
            pltpu.VMEM((tokens, features), jnp.float32),
            pltpu.VMEM((count, tokens, rows), jnp.bfloat16),
            pltpu.SemaphoreType.DMA((count + 3,)),
        ],
        input_output_aliases=aliases,
        compiler_params=params(),
        cost_estimate=LITTLE,
        name="multiply",
    )(*operands, *arrays)


def per_device(
    activations, quant_codes, block_scales, lowrank_down_factor, lowrank_up_factor, cotangent
):
    half = quant_codes.shape[0] // 2
    down_t = lowrank_down_factor.T
    factor = lowrank_scale / math.sqrt(activations.shape[0] * lax.axis_size("fsdp"))
    barrier = lax.optimization_barrier
    join = lambda *arrays: jnp.concatenate(arrays, axis=0)

    def products(pieces, **more):
        return multiply(pieces, activations, down_t, cotangent, lgrad, factor, **more)

    def piece(array, first, dc, key, size=half, offset=0):
        return (array, first, size, offset, (key[0], key[1], dc, key[2]))

    def listed(array, dc, *keys):
        return [piece(array, i * half, dc, key) for i, key in enumerate(keys)]

    own, first = dequantize_shard(quant_codes, block_scales)

    def swap(*arrays):
        return send(join(*arrays), OVER_CORE)

    down1, up1, y1 = send(first, Z_DOWN), send(first, Z_UP), send(own, OVER_Y)
    other_act, other_cot = send(activations, OVER_CORE), send(cotangent, OVER_CORE)
    latent, lgrad, terms_y, kept = local_gradients(
        activations, down_t, lowrank_up_factor, cotangent, other_act, other_cot
    )
    came_y = send(terms_y, OVER_Y)
    down1, up1, y1, kept = barrier((down1, up1, y1, kept))

    down2 = send(join(y1[half:], down1), Z_DOWN)
    x2 = send(join(up1, down1), OVER_X)
    y2 = send(join(down1, up1), OVER_Y)
    rank = down_t.shape[0]
    own_part, next_part, far_part, last_part, up_own, up_away = add_y(kept, terms_y, came_y)
    summed_up = (up_own + send(up_away, OVER_CORE)).astype(jnp.bfloat16)
    came_up = send(join(far_part, summed_up), Z_UP)
    last_part = join(last_part, summed_up)
    swap2 = swap(up1, down1, y1[half:])
    own_keys = [(0, 0, 0), (0, 0, 1)]
    keys = [(1, 0, 0), (3, 0, 0), (0, 1, 0), (0, 1, 1)]
    done = products(
        listed(own, 0, *own_keys)
        + listed(up1, 0, keys[0])
        + listed(down1, 0, keys[1])
        + listed(y1, 0, *keys[2:])
        + listed(swap2, 1, *keys[:2], keys[3]),
        begin=[latent, lowrank_up_factor],
    )
    down2, x2, y2, came_up, own_part, next_part, last_part, done = barrier(
        (down2, x2, y2, came_up, own_part, next_part, last_part, done)
    )

    two = down2[half:]
    quarter = half // 2
    down3 = send(join(down2[:half], last_part), Z_DOWN)
    y3 = send(join(two, x2[:quarter]), OVER_Y)
    x3 = send(join(two, y2[half + quarter :]), OVER_X)
    next_part = next_part + came_up[:rank].astype(jnp.float32)
    up3 = send(join(next_part.astype(jnp.bfloat16), came_up[rank:]), Z_UP)
    swap3 = swap(y2, x2, down2, own, y1[:half])
    keys = [(3, 1, 0), (1, 1, 0), (1, 0, 1), (3, 0, 1), (3, 1, 1), (2, 0, 0)]
    done = products(
        listed(y2, 0, *keys[:2])
        + listed(x2, 0, *keys[2:4])
        + listed(down2, 0, *keys[4:])
        + listed(swap3, 1, *keys, *own_keys, (0, 1, 0)),
        so_far=done,
    )
    x3, y3, down3, up3, came_up, own_part, last_part, done = barrier(
        (x3, y3, down3, up3, came_up, own_part, last_part, done)
    )

    swap4 = swap(y3, x3, down3[:half])
    wide = lambda array: array.astype(jnp.float32)
    tail = slice(half + rank, None)
    up_own = factor * (
        (wide(last_part[rank:]) + wide(up3[rank:])) + (wide(came_up[rank:]) + wide(down3[tail]))
    )
    up_came = send(up_own, OVER_CORE)

    def last(dc, y3, x3, down3, x3_from, down3_from):
        return [
            piece(y3, 0, dc, (2, 1, 0)),
            piece(x3, x3_from, dc, (2, 0, 1)),
            piece(down3, down3_from, dc, (2, 1, 1)),
            piece(y3, half, dc, (1, 1, 1), quarter),
            piece(x3, x3_from + half, dc, (1, 1, 1), quarter, quarter),
        ]

    done = products(last(0, y3, x3, down3, 0, 0), so_far=done)
    x3_from = half + quarter
    projected, gradient, grad_up, grad_down_t = products(
        last(1, swap4, swap4, swap4, x3_from, 2 * x3_from),
        so_far=done,
        end=[up_own, up_came, own_part, up3, down3],
    )
    return (projected, gradient, grad_down_t.T, grad_up)


def solution(mesh):
    in_specs = (
        P(("groups", "fsdp"), None),
        P("fsdp", None),
        P("fsdp", None),
        P("groups", None),
        P("groups", None),
        P(("groups", "fsdp"), None),
    )
    out_specs = (
        P(("groups", "fsdp"), None),
        P(("groups", "fsdp"), None),
        P(("groups", "fsdp"), None),
        P("groups", None),
    )
    small = mesh.shape["groups"] == 2 and mesh.shape["fsdp"] == NZ * 4
    return jax.shard_map(
        per_device if small else per_device_general,
        mesh=mesh,
        in_specs=in_specs,
        out_specs=out_specs,
        check_vma=False,
    )
```

```python
import math

import jax
import jax.numpy as jnp
from jax import lax
from jax.experimental import pallas as pl
from jax.experimental.pallas import tpu as pltpu
from jax.sharding import PartitionSpec as P

BLOCK = 128
AXES = ("groups", "fsdp")

lowrank_scale = 0.5


def weight_transpose(left, right):
    return lax.dot_general(
        left, right, (((1,), (1,)), ((), ())), preferred_element_type=jnp.float32
    )


def leading(left, right):
    return lax.dot_general(
        left, right, (((0,), (0,)), ((), ())), preferred_element_type=jnp.float32
    )


def dequantize(quant_codes, block_scales):
    spread_scales = jnp.repeat(jnp.repeat(block_scales, BLOCK, axis=0), BLOCK, axis=1)
    return (quant_codes.astype(jnp.float32) * spread_scales).astype(jnp.bfloat16)


def per_device_general(
    activations, quant_codes, block_scales, lowrank_down_factor, lowrank_up_factor, cotangent
):
    value_weight = dequantize(quant_codes, block_scales)
    lowrank_hidden = jnp.dot(
        activations, lowrank_down_factor, preferred_element_type=jnp.float32
    ).astype(jnp.bfloat16)
    lowrank_update = lowrank_scale * jnp.dot(
        lowrank_hidden, lowrank_up_factor, preferred_element_type=jnp.float32
    )
    hidden_gradient = weight_transpose(cotangent, lowrank_up_factor).astype(jnp.bfloat16)
    gathered = lax.all_gather(value_weight, "fsdp", axis=0, tiled=True)
    projected = (
        lowrank_update + jnp.dot(activations, gathered, preferred_element_type=jnp.float32)
    ).astype(jnp.bfloat16)
    input_gradient = (
        weight_transpose(cotangent, gathered)
        + lowrank_scale * weight_transpose(hidden_gradient, lowrank_down_factor)
    ).astype(jnp.bfloat16)
    scaling_factor = lowrank_scale / math.sqrt(activations.shape[0] * lax.axis_size("fsdp"))
    grad_down = lax.psum_scatter(
        scaling_factor * leading(activations, hidden_gradient),
        "fsdp",
        scatter_dimension=0,
        tiled=True,
    )
    grad_up = lax.psum(scaling_factor * leading(lowrank_hidden, cotangent), "fsdp")
    return (projected, input_gradient, grad_down, grad_up)


NZ = 4
VMEM_LIMIT = 24 * 1024 * 1024


def pairs_of(move):
    found = []
    for g in range(2):
        for z in range(NZ):
            for y in range(2):
                for c in range(2):
                    to = move(g, z, y, c)
                    found.append((index_of(g, z, y, c), index_of(*to)))
    return found


def index_of(g, z, y, c):
    return ((g * NZ + z) * 2 + y) * 2 + c


OVER_CORE = pairs_of(lambda g, z, y, c: (g, z, y, 1 - c))
OVER_Y = pairs_of(lambda g, z, y, c: (g, z, 1 - y, c))
OVER_X = pairs_of(lambda g, z, y, c: (1 - g, z, y, c))
Z_UP = pairs_of(lambda g, z, y, c: (g, (z + 1) % NZ, y, c))
Z_DOWN = pairs_of(lambda g, z, y, c: (g, (z - 1) % NZ, y, c))
Z_FAR = pairs_of(lambda g, z, y, c: (g, (z + 2) % NZ, y, c))


def position():
    f = lax.axis_index("fsdp")
    return lax.axis_index("groups"), f >> 2, (f >> 1) & 1, f & 1


def send(array, pairs):
    return lax.ppermute(array, AXES, pairs)


def whole():
    return pl.BlockSpec(memory_space=pltpu.VMEM)


def scalars():
    return pl.BlockSpec(memory_space=pltpu.SMEM)


def in_hbm():
    return pl.BlockSpec(memory_space=pltpu.HBM)


def params():
    return pltpu.CompilerParams(vmem_limit_bytes=VMEM_LIMIT)


LITTLE = pl.CostEstimate(flops=1, bytes_accessed=1, transcendentals=0)


def dequantize_shard(quant_codes, block_scales):
    rows, columns = quant_codes.shape
    half = rows // 2

    def kernel(codes_hbm, scales_hbm, own_ref, first_ref, codes_ref, scales_ref, sems):
        g = position()[0]
        scales = pltpu.make_async_copy(scales_hbm, scales_ref, sems.at[0])
        scales.start()
        parts = []
        for i in range(2):
            source = pl.ds(pl.multiple_of(((g + i) & 1) * half, half), half)
            parts.append(
                pltpu.make_async_copy(codes_hbm.at[source, :], codes_ref.at[i], sems.at[i + 1])
            )
            parts[-1].start()
        scales.wait()
        for i in range(2):
            parts[i].wait()
            for k in range(half // BLOCK):
                row = ((g + i) & 1) * (half // BLOCK) + k
                rows_of = slice(k * BLOCK, (k + 1) * BLOCK)
                for j in range(columns // BLOCK):
                    at = slice(j * BLOCK, (j + 1) * BLOCK)
                    block = codes_ref[i, rows_of, at].astype(jnp.float32)
                    block = (block * scales_ref[row, j]).astype(jnp.bfloat16)
                    own_ref[i * half + k * BLOCK : i * half + (k + 1) * BLOCK, at] = block
                    if i == 0:
                        first_ref[rows_of, at] = block

    return pl.pallas_call(
        kernel,
        out_shape=[
            jax.ShapeDtypeStruct((rows, columns), jnp.bfloat16),
            jax.ShapeDtypeStruct((half, columns), jnp.bfloat16),
        ],
        in_specs=[in_hbm(), in_hbm()],
        out_specs=[whole()] * 2,
        scratch_shapes=[
            pltpu.VMEM((2, half, columns), quant_codes.dtype),
            pltpu.SMEM(block_scales.shape, block_scales.dtype),
            pltpu.SemaphoreType.DMA((3,)),
        ],
        compiler_params=pltpu.CompilerParams(vmem_limit_bytes=53 * 1024 * 1024),
        cost_estimate=pl.CostEstimate(flops=20000000000, bytes_accessed=1, transcendentals=0),
        name="dequantize",
    )(quant_codes, block_scales)


def local_gradients(activations, down_t, up, cotangent, other_act, other_cot):
    tokens, width = activations.shape
    rank, features = up.shape
    chips = NZ * 2
    chunk = width // chips
    part = chunk // 2

    def kernel(
        act_hbm, down_hbm, up_hbm, cot_hbm, other_hbm, other_cot_hbm, latent_ref,
        lgrad_ref, message_ref, kept_ref, act_ref, down_ref, up_ref, cot_ref, other_ref,
        other_cot_ref, total, lgrad_t, other_t, sums, sems,
    ):
        _, _, y, c = position()
        copies = []

        def fetch(source, target):
            copies.append(pltpu.make_async_copy(source, target, sems.at[len(copies)]))
            copies[-1].start()

        for source, target in (
            (up_hbm, up_ref), (cot_hbm, cot_ref), (other_cot_hbm, other_cot_ref),
        ):
            fetch(source, target)
        for i in range(chips):
            at = slice(i * chunk, (i + 1) * chunk)
            mine = pl.ds(pl.multiple_of((2 * i + c) * part, part), part)
            fetch(act_hbm.at[:, at], act_ref.at[i])
            fetch(other_hbm.at[:, mine], other_ref.at[i])
            fetch(down_hbm.at[:, at], down_ref.at[i])
        for copy in copies[:3]:
            copy.wait()
        lgrad_ref[...] = weight_transpose(cot_ref[...], up_ref[...]).astype(jnp.bfloat16)
        lgrad_t[...] = weight_transpose(up_ref[...], cot_ref[...]).astype(jnp.bfloat16)
        other_t[...] = weight_transpose(up_ref[...], other_cot_ref[...]).astype(jnp.bfloat16)
        mine = pl.ds(pl.multiple_of(c * part, part), part)
        for i in range(chips):
            for copy in copies[3 * i + 3 : 3 * i + 6]:
                copy.wait()
            sums[i % 2, i // 2 * rank : (i // 2 + 1) * rank, :] = jnp.dot(
                lgrad_t[...], act_ref[i, :, mine], preferred_element_type=jnp.float32
            ) + jnp.dot(other_t[...], other_ref[i], preferred_element_type=jnp.float32)
            latent = weight_transpose(act_ref[i], down_ref[i])
            if i == 0:
                total[...] = latent
            else:
                total[...] += latent
        message_ref[: NZ * rank, :] = sums[1 - y].astype(jnp.bfloat16)
        kept_ref[...] = sums[y]
        latent_ref[...] = total[...].astype(jnp.bfloat16)
        message_ref[NZ * rank :, :] = leading(latent_ref[...], cot_ref[...]).astype(jnp.bfloat16)

    bf16 = jnp.bfloat16
    return pl.pallas_call(
        kernel,
        out_shape=[
            jax.ShapeDtypeStruct((tokens, rank), bf16),
            jax.ShapeDtypeStruct((tokens, rank), bf16),
            jax.ShapeDtypeStruct(((NZ + 1) * rank, part), bf16),
            jax.ShapeDtypeStruct((NZ * rank, part), jnp.float32),
        ],
        in_specs=[in_hbm()] * 6,
        out_specs=[whole()] * 4,
        scratch_shapes=[
            pltpu.VMEM((chips, tokens, chunk), bf16),
            pltpu.VMEM((chips, rank, chunk), bf16),
            pltpu.VMEM((rank, features), bf16),
            pltpu.VMEM((tokens, features), bf16),
            pltpu.VMEM((chips, tokens, part), bf16),
            pltpu.VMEM((tokens, features), bf16),
            pltpu.VMEM((tokens, rank), jnp.float32),
            pltpu.VMEM((rank, tokens), bf16),
            pltpu.VMEM((rank, tokens), bf16),
            pltpu.VMEM((2, NZ * rank, part), jnp.float32),
            pltpu.SemaphoreType.DMA((3 * chips + 3,)),
        ],
        compiler_params=pltpu.CompilerParams(vmem_limit_bytes=24 * 1024 * 1024),
        cost_estimate=LITTLE,
        name="local_gradients",
    )(activations, down_t, up, cotangent, other_act, other_cot)


def add_y(kept, sent, came):
    rows, part = kept.shape
    rank = rows // NZ
    fold = rank // 2
    kinds = [jnp.float32, jnp.float32, jnp.bfloat16, jnp.bfloat16]

    def kernel(kept_ref, sent_ref, came_ref, *out_refs):
        _, z, _, c = position()
        f32 = jnp.float32
        for shift in range(NZ):
            at = pl.ds(pl.multiple_of(lax.rem(z + shift, NZ) * rank, rank), rank)
            summed = kept_ref[at, :] + came_ref[at, :].astype(f32)
            out_refs[shift][...] = summed.astype(kinds[shift])
        term = sent_ref[rows:, :].astype(f32) + came_ref[rows:, :].astype(f32)
        low, high = term[:, : part // 2], term[:, part // 2 :]
        for core, ref in enumerate(out_refs[NZ:]):
            half = jnp.where(c == core, low, high)
            ref[:, : part // 2] = half[:fold]
            ref[:, part // 2 :] = half[fold:]

    return pl.pallas_call(
        kernel,
        out_shape=[jax.ShapeDtypeStruct((rank, part), kind) for kind in kinds]
        + [jax.ShapeDtypeStruct((fold, part), jnp.float32)] * 2,
        in_specs=[whole()] * 3,
        out_specs=[whole()] * (NZ + 2),
        compiler_params=params(),
        cost_estimate=pl.CostEstimate(flops=10000000000, bytes_accessed=1, transcendentals=0),
        name="add_y",
    )(kept, sent, came)


def multiply(
    pieces, activations, down_t, cotangent, lgrad, factor, begin=None, so_far=None, end=None
):
    tokens, width = activations.shape
    features = cotangent.shape[1]
    arrays = []
    for array, *_ in pieces:
        if not any(array is other for other in arrays):
            arrays.append(array)
    where = [next(i for i, a in enumerate(arrays) if a is array) for array, *_ in pieces]
    count = len(pieces)
    rows = width // (NZ * 2 * 2 * 2)

    def kernel(*refs):
        refs = list(refs)
        act_ref, down_ref, cot_ref, lgrad_ref, one_ref, two_ref = refs[:6]
        del refs[:6]
        if end is not None:
            terms = refs[:5]
            del refs[:5]
        array_refs = refs[: len(arrays)]
        del refs[: len(arrays)]
        out_ref, grad_ref = refs[:2]
        sums, grads, out_sems = refs[-3:]
        g, z, y, c = position()
        columns, weights, going = [], [], []
        for p, (_, first, size, offset, (dz, dy, dc, dh)) in enumerate(pieces):
            chip = lax.rem(z + (NZ - dz), NZ) * 2 + (1 - y if dy else y)
            device = chip * 2 + (1 - c if dc else c)
            start = (device * 2 + (1 - g if dh else g)) * rows + offset
            columns.append(pl.ds(pl.multiple_of(start, BLOCK), size))
            weights.append(array_refs[where[p]].at[first : first + size, :])

        def give(source, target):
            going.append(pltpu.make_async_copy(source, target, out_sems.at[len(going)]))
            going[-1].start()

        def backward():
            for p in range(count):
                held = grads.at[p, :, : pieces[p][2]]
                held[...] = (
                    weight_transpose(cot_ref[...], weights[p][...])
                    + lowrank_scale
                    * jnp.dot(
                        lgrad_ref[...], down_ref[:, columns[p]], preferred_element_type=jnp.float32
                    )
                ).astype(jnp.bfloat16)
                give(held, grad_ref.at[:, columns[p]])

        def forward():
            if begin is not None:
                sums[...] = lowrank_scale * jnp.dot(
                    one_ref[...], two_ref[...], preferred_element_type=jnp.float32
                )
            else:
                sums[...] = one_ref[...]
            for p in range(count):
                sums[...] += jnp.dot(
                    act_ref[:, columns[p]], weights[p][...], preferred_element_type=jnp.float32
                )

        if end is None:
            backward()
            forward()
            out_ref[...] = sums[...]
        else:
            up_out, down_out, rounded, up_sum, down_sum = refs[2:7]
            rank = down_ref.shape[0]
            part = features // 2
            for ref, core in zip(terms[:2], (c, 1 - c), strict=True):
                at = pl.ds(pl.multiple_of(core * part, part), part)
                up_sum[: rank // 2, at] = ref[:, :part]
                up_sum[rank // 2 :, at] = ref[:, part:]
            give(up_sum, up_out)
            down_sum[...] = factor * (
                terms[2][...]
                + terms[3][:rank, :].astype(jnp.float32)
                + terms[4][rows : rows + rank, :].astype(jnp.float32)
            )
            give(down_sum, down_out)
            forward()
            rounded[...] = sums[...].astype(jnp.bfloat16)
            give(rounded, out_ref)
            backward()
        for copy in going:
            copy.wait()

    operands = [activations, down_t, cotangent, lgrad]
    specs = [whole()] * 4
    out_shape = [
        jax.ShapeDtypeStruct((tokens, features), jnp.float32 if end is None else jnp.bfloat16),
        jax.ShapeDtypeStruct((tokens, width), jnp.bfloat16),
    ]
    out_specs = [whole() if end is None else in_hbm(), in_hbm()]
    scratch = [] if end is None else [pltpu.VMEM((tokens, features), jnp.bfloat16)]
    aliases = {}
    if begin is not None:
        operands += begin
        specs += [whole()] * 2
    else:
        operands += so_far
        specs += [whole(), in_hbm()]
        aliases = {5: 1}
    if end is not None:
        operands += end
        specs += [whole()] * 5
        for _ in range(2):
            out_shape.append(jax.ShapeDtypeStruct((down_t.shape[0], features), jnp.float32))
            out_specs.append(in_hbm())
            scratch.append(pltpu.VMEM((down_t.shape[0], features), jnp.float32))
    return pl.pallas_call(
        kernel,
        out_shape=out_shape,
        in_specs=specs + [whole()] * len(arrays),
        out_specs=out_specs,
        scratch_shapes=scratch
        + [
            pltpu.VMEM((tokens, features), jnp.float32),
            pltpu.VMEM((count, tokens, rows), jnp.bfloat16),
            pltpu.SemaphoreType.DMA((count + 3,)),
        ],
        input_output_aliases=aliases,
        compiler_params=params(),
        cost_estimate=LITTLE,
        name="multiply",
    )(*operands, *arrays)


def per_device(
    activations, quant_codes, block_scales, lowrank_down_factor, lowrank_up_factor, cotangent
):
    half = quant_codes.shape[0] // 2
    down_t = lowrank_down_factor.T
    factor = lowrank_scale / math.sqrt(activations.shape[0] * lax.axis_size("fsdp"))
    barrier = lax.optimization_barrier
    join = lambda *arrays: jnp.concatenate(arrays, axis=0)

    def products(pieces, **more):
        return multiply(pieces, activations, down_t, cotangent, lgrad, factor, **more)

    def piece(array, first, dc, key, size=half, offset=0):
        return (array, first, size, offset, (key[0], key[1], dc, key[2]))

    def listed(array, dc, *keys):
        return [piece(array, i * half, dc, key) for i, key in enumerate(keys)]

    own, first = dequantize_shard(quant_codes, block_scales)

    def swap(*arrays):
        return send(join(*arrays), OVER_CORE)

    down1, up1, y1 = send(first, Z_DOWN), send(first, Z_UP), send(own, OVER_Y)
    other_act, other_cot = send(activations, OVER_CORE), send(cotangent, OVER_CORE)
    latent, lgrad, terms_y, kept = local_gradients(
        activations, down_t, lowrank_up_factor, cotangent, other_act, other_cot
    )
    came_y = send(terms_y, OVER_Y)
    down1, up1, y1, kept = barrier((down1, up1, y1, kept))

    down2 = send(join(y1[half:], down1), Z_DOWN)
    x2 = send(join(up1, down1), OVER_X)
    y2 = send(join(down1, up1), OVER_Y)
    rank = down_t.shape[0]
    own_part, next_part, far_part, last_part, up_own, up_away = add_y(kept, terms_y, came_y)
    summed_up = (up_own + send(up_away, OVER_CORE)).astype(jnp.bfloat16)
    came_up = send(join(far_part, summed_up), Z_UP)
    last_part = join(last_part, summed_up)
    swap2 = swap(up1, down1, y1[half:])
    own_keys = [(0, 0, 0), (0, 0, 1)]
    keys = [(1, 0, 0), (3, 0, 0), (0, 1, 0), (0, 1, 1)]
    done = products(
        listed(own, 0, *own_keys)
        + listed(up1, 0, keys[0])
        + listed(down1, 0, keys[1])
        + listed(y1, 0, *keys[2:])
        + listed(swap2, 1, *keys[:2], keys[3]),
        begin=[latent, lowrank_up_factor],
    )
    down2, x2, y2, came_up, own_part, next_part, last_part, done = barrier(
        (down2, x2, y2, came_up, own_part, next_part, last_part, done)
    )

    two = down2[half:]
    quarter = half // 2
    down3 = send(join(down2[:half], last_part), Z_DOWN)
    y3 = send(join(two, x2[:quarter]), OVER_Y)
    x3 = send(join(two, y2[half + quarter :]), OVER_X)
    next_part = next_part + came_up[:rank].astype(jnp.float32)
    up3 = send(join(next_part.astype(jnp.bfloat16), came_up[rank:]), Z_UP)
    swap3 = swap(y2, x2, down2, own, y1[:half])
    keys = [(3, 1, 0), (1, 1, 0), (1, 0, 1), (3, 0, 1), (3, 1, 1), (2, 0, 0)]
    done = products(
        listed(y2, 0, *keys[:2])
        + listed(x2, 0, *keys[2:4])
        + listed(down2, 0, *keys[4:])
        + listed(swap3, 1, *keys, *own_keys, (0, 1, 0)),
        so_far=done,
    )
    x3, y3, down3, up3, came_up, own_part, last_part, done = barrier(
        (x3, y3, down3, up3, came_up, own_part, last_part, done)
    )

    swap4 = swap(y3, x3, down3[:half])
    wide = lambda array: array.astype(jnp.float32)
    tail = slice(half + rank, None)
    up_own = factor * (
        (wide(last_part[rank:]) + wide(up3[rank:])) + (wide(came_up[rank:]) + wide(down3[tail]))
    )
    up_came = send(up_own, OVER_CORE)

    def last(dc, y3, x3, down3, x3_from, down3_from):
        return [
            piece(y3, 0, dc, (2, 1, 0)),
            piece(x3, x3_from, dc, (2, 0, 1)),
            piece(down3, down3_from, dc, (2, 1, 1)),
            piece(y3, half, dc, (1, 1, 1), quarter),
            piece(x3, x3_from + half, dc, (1, 1, 1), quarter, quarter),
        ]

    done = products(last(0, y3, x3, down3, 0, 0), so_far=done)
    x3_from = half + quarter
    projected, gradient, grad_up, grad_down_t = products(
        last(1, swap4, swap4, swap4, x3_from, 2 * x3_from),
        so_far=done,
        end=[up_own, up_came, own_part, up3, down3],
    )
    return (projected, gradient, grad_down_t.T, grad_up)


def solution(mesh):
    in_specs = (
        P(("groups", "fsdp"), None),
        P("fsdp", None),
        P("fsdp", None),
        P("groups", None),
        P("groups", None),
        P(("groups", "fsdp"), None),
    )
    out_specs = (
        P(("groups", "fsdp"), None),
        P(("groups", "fsdp"), None),
        P(("groups", "fsdp"), None),
        P("groups", None),
    )
    small = mesh.shape["groups"] == 2 and mesh.shape["fsdp"] == NZ * 4
    return jax.shard_map(
        per_device if small else per_device_general,
        mesh=mesh,
        in_specs=in_specs,
        out_specs=out_specs,
        check_vma=False,
    )
```
